32 devices in a mesh: frame: 8 (over z, x), head: 4 (over y, core).
Axes of the slice: x: 2, y: 2, z: 4, core: 2. Of those that a mesh axis runs over, the one named last changes fastest.
Arguments:
- video_queries: bfloat16 [6144, 3072], P(('frame', 'head')), may hold values from -16 to 16
- video_keys: bfloat16 [6144, 3072], P(('frame', 'head')), may hold values from -16 to 16
- video_values: bfloat16 [6144, 3072], P(('frame', 'head')), may hold values from -6 to 6
- text_keys: bfloat16 [256, 3072], P('frame', 'head'), may hold values from -15 to 15
- text_values: bfloat16 [256, 3072], P('frame', 'head'), may hold values from -6 to 6
- kept_tiles: int32 [48, 12], P('frame'), may hold values from 0 to 47, as said below
- kept_count: int32 [48], P('frame'), may hold values from 1 to 12
- text_len: int32 [1], replicated, may hold values from 128 to 256
Outputs:
- attention_out: bfloat16 [6144, 3072], P(('frame', 'head'))
The draws below stay inside these ranges and needn't reach their ends.
Inputs may be any that keep to these rules, and one draw needn't show every extreme that they name: `kept_tiles`: each row holds 12 distinct tiles; its first entry is the query tile itself, and every entry lies in the query tile's slab or in the slab just before or after it on the loop, where slab 8 - 1 is next to slab 0.
All inputs are finite; a program needn't handle non-finite values.
Results may differ from the reference program's by a relative error of at most 0.003.
Values may be sent and summed in bfloat16 or wider, within the bound.
No kernel may reach another device: no remote copies, remote signals or barrier semaphores. Data moves between devices by JAX's collectives and lax.ppermute only.
A program may use at most 128 MiB of HBM per device.

```python
import math
import jax
import jax.numpy as jnp
from jax import lax

HEADS = 24
HD = 128
TILE = 128
TPD = 6
TXT = 256
KEEP = 12
SLABS = 8
QTILES = 48
TOKENS = 6144


def lead_strength(slab_number):
    return jnp.where(slab_number % 3 == 0, 20.0, jnp.where(slab_number % 3 == 1, 40.0, 70.0))


def key_field(key, spread, lead):
    row_total = TOKENS
    column_total = HEADS * HD
    part_a = jax.random.fold_in(jax.random.fold_in(key, 101), 0)
    part_c = jax.random.fold_in(jax.random.fold_in(key, 101), 2)
    part_d = jax.random.fold_in(jax.random.fold_in(key, 101), 3)
    part_e = jax.random.fold_in(jax.random.fold_in(key, 101), 4)
    drawn = jnp.clip(jax.random.normal(part_a, (row_total, column_total), jnp.float32), -6.0, 6.0)
    row_scale = jnp.exp(jax.random.uniform(part_c, (row_total, 1), jnp.float32, -spread, spread))
    field = 1.5 * drawn * row_scale
    position = jnp.arange(row_total) % (TILE * TPD)
    slab_number = jnp.arange(row_total) // (TILE * TPD)
    strength = lead_strength(slab_number)
    signs = jnp.where(jax.random.bernoulli(part_d, 0.5, (row_total, column_total)), 1.0, -1.0)
    magnitude = jax.random.uniform(part_e, (row_total, column_total), jnp.float32, 0.7, 1.0) * 12.0
    leading = signs * magnitude
    factor = 1.0 - 2.0 / (0.73 * strength * math.sqrt(HD))
    is_lead = (position == 1)[:, None] & (lead > 0)
    is_twin = (position == 2)[:, None] & (lead > 0)
    field = jnp.where(is_lead, leading, field)
    field = jnp.where(is_twin, jnp.roll(leading, 1, axis=0) * factor[:, None], field)
    return field


def tile_plan(key):
    slab_count = QTILES // TPD
    part_a, part_b, part_c, part_d = jax.random.split(jax.random.fold_in(key, 202), 4)
    tile_index = jnp.arange(QTILES, dtype=jnp.int32)
    home_slab = tile_index // TPD
    busy_slab = (jax.random.randint(part_a, (slab_count,), 0, 4) == 0).at[0].set(True)
    busy_row = busy_slab[home_slab]
    high = jax.random.randint(part_b, (QTILES,), KEEP // 2, KEEP + 1)
    low = jax.random.randint(part_c, (QTILES,), 1, KEEP // 4 + 2)
    live_counts = jnp.where(busy_row, high, low)
    live_counts = live_counts.at[0].set(KEEP).at[QTILES - 1].set(1)
    window = 3 * TPD
    column = jnp.arange(window, dtype=jnp.int32)
    cand_slab = (home_slab[:, None] + column[None, :] // TPD - 1 + slab_count) % slab_count
    cand_tile = cand_slab * TPD + column[None, :] % TPD
    ranking = jax.random.randint(part_d, (QTILES, window), 0, 1 << 20) * window + column[None, :]
    own_column = TPD + tile_index % TPD
    ranking = jnp.where(column[None, :] == own_column[:, None], -1, ranking)
    order = jnp.argsort(ranking, axis=1, stable=True)[:, :KEEP]
    tile_lists = jnp.take_along_axis(cand_tile, order, axis=1)
    return (tile_lists.astype(jnp.int32), live_counts.astype(jnp.int32))


def draw_video_keys(key, part):
    spread, lead = (0.0, 0.0)
    field = key_field(key, spread, lead)
    return field.astype(jnp.bfloat16)


def draw_video_queries(key, part):
    spread, lead = (0.0, 0.0)
    field = key_field(key, spread, lead)
    key = jax.random.fold_in(key, 7)
    row_total = TOKENS
    column_total = HEADS * HD
    part_a = jax.random.fold_in(key, 0)
    part_c = jax.random.fold_in(key, 2)
    drawn = jnp.clip(jax.random.normal(part_a, (row_total, column_total), jnp.float32), -6.0, 6.0)
    row_scale = jnp.exp(jax.random.uniform(part_c, (row_total, 1), jnp.float32, -spread, spread))
    own_values = drawn * row_scale
    position = jnp.arange(row_total) % (TILE * TPD)
    slab_number = jnp.arange(row_total) // (TILE * TPD)
    strength = lead_strength(slab_number)
    is_lead = (position == 1)[:, None] & (lead > 0)
    queries = jnp.where(is_lead, field * (strength[:, None] / 144.0), own_values)
    return queries.astype(jnp.bfloat16)


def draw_kept_tiles(key, part):
    tile_lists, live_counts = tile_plan(key)
    return tile_lists


def draw_kept_count(key, part):
    tile_lists, live_counts = tile_plan(key)
    return live_counts


def steps_of(key, dims, pieces, least, largest):
    level, own = 1.0, jax.random.fold_in(key, 6)
    for axis_at, blocks in pieces:
        steps = jnp.exp(jax.random.uniform(jax.random.fold_in(own, axis_at), (blocks,), jnp.float32, least / len(pieces), largest / len(pieces)))
        level = level * jnp.repeat(steps, dims[axis_at] // blocks).reshape([-1 if axis == axis_at else 1 for axis in range(len(dims))])
    return level


def gaussian(stream_key, extent, width, bound, cuts=(), kind=jnp.bfloat16):
    values = width * jax.random.normal(stream_key, extent, jnp.float32)
    if cuts:
        values = values * steps_of(stream_key, extent, cuts, -0.22, 0.18)
    return jnp.clip(values, -bound, bound).astype(kind)


def setup_inputs(seed: int = 0) -> dict:
    streams_of = jax.random.split(jax.random.key(seed), 9)
    video_queries = draw_video_queries(jax.random.fold_in(streams_of[8], 71), 0)
    video_keys = draw_video_keys(jax.random.fold_in(streams_of[8], 71), 0)
    video_values = gaussian(streams_of[2], (TOKENS, HEADS * HD), 1.0, 6.0, ((0, 32),))
    text_keys = gaussian(streams_of[3], (TXT, HEADS * HD), 2.5, 15.0, ((0, 8), (1, 4)))
    text_values = gaussian(streams_of[4], (TXT, HEADS * HD), 1.0, 6.0, ((0, 8), (1, 4)))
    kept_tiles = draw_kept_tiles(jax.random.fold_in(streams_of[8], 71), 0)
    kept_count = draw_kept_count(jax.random.fold_in(streams_of[8], 71), 0)
    text_len = jax.random.randint(streams_of[7], (1,), TXT // 2, TXT + 1).astype(jnp.int32)
    return {"video_queries": video_queries, "video_keys": video_keys, "video_values": video_values, "text_keys": text_keys, "text_values": text_values, "kept_tiles": kept_tiles, "kept_count": kept_count, "text_len": text_len}


def tile_mask(tile_lists, live_counts, slab_index, slab_count, tile_count):
    key_ids = ((slab_index + slab_count) % slab_count * tile_count + jnp.arange(tile_count, dtype=jnp.int32)).astype(jnp.int32)
    slot_live = jnp.arange(tile_lists.shape[1], dtype=jnp.int32)[None, :] < live_counts[:, None]
    matches = (tile_lists[:, :, None] == key_ids[None, None, :]) & slot_live[:, :, None]
    return jnp.any(matches, axis=1)

def token_mask(tile_allow, tile_size):
    query_tiles, key_tiles = tile_allow.shape
    spread_out = jnp.broadcast_to(tile_allow[:, None, :, None], (query_tiles, tile_size, key_tiles, tile_size))
    return spread_out.reshape(query_tiles * tile_size, key_tiles * tile_size)

def partial_attention(queries, keys_here, values, allowed, head_dim):
    row_count = queries.shape[0]
    feature_width = queries.shape[1]
    heads_here = feature_width // head_dim
    query_heads = jnp.transpose(queries.reshape(row_count, heads_here, head_dim), (1, 0, 2))
    key_heads = jnp.transpose(keys_here.reshape(keys_here.shape[0], heads_here, head_dim), (1, 0, 2))
    value_heads = jnp.transpose(values.reshape(values.shape[0], heads_here, head_dim), (1, 0, 2))
    scale = 1.0 / math.sqrt(head_dim)

    def one_head(operands):
        query_one, key_one, value_one = operands
        scores = jnp.dot(query_one, key_one.T, preferred_element_type=jnp.float32) * scale
        masked = jnp.where(allowed, scores, -1e+30)
        row_max = lax.optimization_barrier(jnp.max(masked, axis=1))
        weights = jnp.where(allowed, jnp.exp(masked - row_max[:, None]), 0.0)
        row_sum = lax.optimization_barrier(jnp.sum(weights, axis=1))
        weighted = jnp.dot(weights.astype(jnp.bfloat16), value_one, preferred_element_type=jnp.float32)
        return (weighted, row_max, row_sum)
    weighted, row_max, row_sum = lax.map(one_head, (query_heads, key_heads, value_heads))
    return (jnp.transpose(weighted, (1, 0, 2)).reshape(row_count, feature_width), row_max.T, row_sum.T)

def combine(partials, head_dim):
    row_count, feature_width = partials[0][0].shape
    heads_here = feature_width // head_dim
    overall = partials[0][1]
    for member in partials[1:]:
        overall = jnp.maximum(overall, member[1])
    numerator = jnp.zeros((row_count, heads_here, head_dim), jnp.float32)
    denominator = jnp.zeros((row_count, heads_here), jnp.float32)
    for weighted, row_max, row_sum in partials:
        factor = jnp.exp(row_max - overall)
        numerator = numerator + weighted.reshape(row_count, heads_here, head_dim) * factor[:, :, None]
        denominator = denominator + row_sum * factor
    return (numerator / denominator[:, :, None]).reshape(row_count, feature_width).astype(jnp.bfloat16)

def reference(video_queries, video_keys, video_values, text_keys, text_values, kept_tiles, kept_count, text_len):
    row_count = TILE * TPD
    feature_width = HEADS * HD
    query_slabs = video_queries.reshape(SLABS, row_count, feature_width)
    key_slabs = video_keys.reshape(SLABS, row_count, feature_width)
    value_slabs = video_values.reshape(SLABS, row_count, feature_width)
    tile_lists = kept_tiles.reshape(SLABS, TPD, KEEP)
    live_counts = kept_count.reshape(SLABS, TPD)
    text_live = jnp.arange(TXT, dtype=jnp.int32) < text_len[0]
    text_allow = jnp.broadcast_to(text_live[None, :], (row_count, TXT))

    def one_slab(slab_index):
        before = (slab_index + SLABS - 1) % SLABS
        after_index = (slab_index + 1) % SLABS
        lists_here = tile_lists[slab_index]
        counts_here = live_counts[slab_index]
        queries = query_slabs[slab_index]
        own_allow = jnp.concatenate([token_mask(tile_mask(lists_here, counts_here, slab_index, SLABS, TPD), TILE), text_allow], axis=1)
        own_part = partial_attention(queries, jnp.concatenate([key_slabs[slab_index], text_keys], axis=0), jnp.concatenate([value_slabs[slab_index], text_values], axis=0), own_allow, HD)
        before_part = partial_attention(queries, key_slabs[before], value_slabs[before], token_mask(tile_mask(lists_here, counts_here, slab_index - 1, SLABS, TPD), TILE), HD)
        after_part = partial_attention(queries, key_slabs[after_index], value_slabs[after_index], token_mask(tile_mask(lists_here, counts_here, slab_index + 1, SLABS, TPD), TILE), HD)
        return combine([own_part, before_part, after_part], HD)
    mixed = lax.map(one_slab, jnp.arange(SLABS, dtype=jnp.int32))
    return mixed.reshape(TOKENS, feature_width)
```

```python
import functools
import math

import jax
import jax.numpy as jnp
from jax import lax
from jax.experimental import pallas as pl
from jax.experimental.pallas import tpu as pltpu
from jax.sharding import PartitionSpec as P

HD = 128
TILE = 128
AXES = ("frame", "head")
SCALE = math.log2(math.e) / math.sqrt(HD)
LOW = -1e30
NT = (((1,), (1,)), ((), ()))
SMEM = pl.BlockSpec(memory_space=pltpu.SMEM)
PARAMS = pltpu.CompilerParams(vmem_limit_bytes=48 << 20)


def group(queries, keys, values_t, biases):
    scores = lax.dot_general(keys, queries, NT, preferred_element_type=jnp.float32)
    key_tiles, query_tiles = keys.shape[0] // TILE, queries.shape[0] // TILE
    tops, totals, weights = [], [], []
    for t in range(query_tiles):
        blocks = [
            scores[u * TILE : (u + 1) * TILE, t * TILE : (t + 1) * TILE] + biases[u][t]
            for u in range(key_tiles)
        ]
        top = functools.reduce(jnp.maximum, blocks)
        top = jnp.max(top, axis=0, keepdims=True)
        parts = [jnp.exp2((block - top) * SCALE) for block in blocks]
        total = functools.reduce(jnp.add, parts)
        tops.append(top)
        totals.append(jnp.sum(total, axis=0, keepdims=True))
        weights.append(jnp.concatenate([p.astype(jnp.bfloat16) for p in parts], axis=0))
    weighted = jnp.dot(
        values_t, jnp.concatenate(weights, axis=1), preferred_element_type=jnp.float32
    )
    return weighted, jnp.concatenate(tops, axis=1), jnp.concatenate(totals, axis=1)


def merge(one, two):
    top = jnp.maximum(one[1], two[1])
    first, second = jnp.exp2((one[1] - top) * SCALE), jnp.exp2((two[1] - top) * SCALE)
    return one[0] * first + two[0] * second, top, one[2] * first + two[2] * second


def local_kernel(
    tiles, bias, q_ref, k_ref, v_ref, tk_ref, tv_ref, tb_ref, sum_ref, stat_ref
):
    side = pl.program_id(1)
    rows = tiles * TILE
    own = pl.ds(pl.multiple_of(side * rows, rows), rows)
    other = pl.ds(pl.multiple_of((1 - side) * rows, rows), rows)
    queries = q_ref[...]
    at = lambda t, u: bias[(side * tiles + t) * 3 * tiles + u]
    text_tiles = tk_ref.shape[0] // TILE
    own_bias = [[at(t, u) for t in range(tiles)] for u in range(tiles)]
    own_bias += [[tb_ref[j * TILE : (j + 1) * TILE, :]] * tiles for j in range(text_tiles)]
    mine = group(
        queries,
        jnp.concatenate([k_ref[own, :], tk_ref[...]], axis=0),
        jnp.concatenate([v_ref[own, :], tv_ref[...]], axis=0).T,
        own_bias,
    )
    theirs = group(
        queries,
        k_ref[other, :],
        v_ref[other, :].T,
        [[at(t, tiles + u) for t in range(tiles)] for u in range(tiles)],
    )
    weighted, top, total = merge(mine, theirs)
    sum_ref[0, 0] = weighted
    stat_ref[0, 0, 0:1, :] = top
    stat_ref[0, 0, 1:2, :] = total


def halo_kernel(tiles, bias, q_ref, k_ref, v_ref, sum_ref, stat_ref, out_ref):
    side = pl.program_id(1)
    at = lambda t, u: bias[(side * tiles + t) * 3 * tiles + u]

    def run(keys, values):
        far = group(
            q_ref[...],
            keys,
            values.T,
            [[at(t, 2 * tiles + u) for t in range(tiles)] for u in range(tiles)],
        )
        near = (sum_ref[0, 0], stat_ref[0, 0, 0:1, :], stat_ref[0, 0, 1:2, :])
        weighted, _, total = merge(near, far)
        out_ref[...] = (weighted / total).T.astype(out_ref.dtype)

    run(k_ref[0], v_ref[0])


def local_attention(tiles, bias, q, k, v, text_k, text_v, text_bias):
    heads, rows, text = q.shape[1] // HD, tiles * TILE, text_k.shape[0]
    whole = pl.BlockSpec((2 * rows, HD), lambda h, s: (0, h))
    text_block = pl.BlockSpec((text, HD), lambda h, s: (0, h))
    return pl.pallas_call(
        functools.partial(local_kernel, tiles),
        grid=(heads, 2),
        in_specs=[
            SMEM,
            pl.BlockSpec((rows, HD), lambda h, s: (s, h)),
            whole,
            whole,
            text_block,
            text_block,
            pl.BlockSpec((text, TILE), lambda h, s: (0, 0)),
        ],
        out_specs=[
            pl.BlockSpec((1, 1, HD, rows), lambda h, s: (h, s, 0, 0)),
            pl.BlockSpec((1, 1, 2, rows), lambda h, s: (h, s, 0, 0)),
        ],
        out_shape=[
            jax.ShapeDtypeStruct((heads, 2, HD, rows), jnp.float32),
            jax.ShapeDtypeStruct((heads, 2, 2, rows), jnp.float32),
        ],
        compiler_params=PARAMS,
    )(bias, q, k, v, text_k, text_v, text_bias)


def halo_attention(tiles, bias, q, k, v, sums, stats):
    heads, rows = q.shape[1] // HD, tiles * TILE
    block = pl.BlockSpec((rows, HD), lambda h, s: (s, h))
    far = pl.BlockSpec((1, rows, HD), lambda h, s: (s, 0, h))
    return pl.pallas_call(
        functools.partial(halo_kernel, tiles),
        grid=(heads, 2),
        in_specs=[
            SMEM,
            block,
            far,
            far,
            pl.BlockSpec((1, 1, HD, rows), lambda h, s: (h, s, 0, 0)),
            pl.BlockSpec((1, 1, 2, rows), lambda h, s: (h, s, 0, 0)),
        ],
        out_specs=block,
        out_shape=jax.ShapeDtypeStruct(q.shape, jnp.bfloat16),
        compiler_params=PARAMS,
    )(bias, q, k, v, sums, stats)


def kept_mask(lists, counts, slab, slabs, tiles):
    ids = (slab + slabs) % slabs * tiles + jnp.arange(tiles, dtype=jnp.int32)
    live = jnp.arange(lists.shape[1], dtype=jnp.int32)[None, :] < counts[:, None]
    return jnp.any((lists[:, :, None] == ids[None, None, :]) & live[:, :, None], axis=1)


def body(queries, keys, values, text_keys, text_values, lists, counts, text_len):
    slabs, heads = lax.axis_size("frame"), lax.axis_size("head")
    slab, pair, side = lax.axis_index("frame"), lax.axis_index("frame") // 2, lax.axis_index("frame") % 2
    ways, pairs = 2 * heads, slabs // 2
    tiles = lists.shape[0]
    rows, width = queries.shape
    part = width // ways
    count = slabs * heads
    groups = [list(range(ways * i, ways * (i + 1))) for i in range(pairs)]

    def shifted(x, by):
        return lax.ppermute(x, AXES, [(i, (i + by * ways) % count) for i in range(count)])

    def swapped(x):
        flip = lambda i: i // ways * ways + (i + heads) % ways
        return lax.ppermute(x, AXES, [(i, flip(i)) for i in range(count)])

    def exchange(x):
        return lax.all_to_all(
            x, AXES, split_axis=0, concat_axis=0, tiled=True, axis_index_groups=groups
        )

    def spread(x):
        x = x.reshape(rows, heads, 2, part).transpose(2, 1, 0, 3)
        return exchange(x.reshape(ways, rows, part))

    toward, away = jnp.where(side == 0, 1, -1), jnp.where(side == 0, -1, 1)
    mask = jnp.concatenate(
        [kept_mask(lists, counts, slab + by, slabs, tiles) for by in (0, toward, away)], axis=1
    ).astype(jnp.bfloat16)

    text_rows = text_keys.shape[0]
    text = jnp.stack([text_keys, text_values]).reshape(2, text_rows, 2, part)
    send = lax.dynamic_index_in_dim(text, 1 - side, 2, keepdims=False)
    keep = lax.dynamic_index_in_dim(text, side, 2, keepdims=False)
    flat = mask.reshape(1, 1, -1)
    row = jnp.pad(flat, ((0, 0), (0, text_rows - 1), (0, part - flat.shape[2])))
    got = swapped(jnp.concatenate([send, row], axis=0))
    got_mask = got[2, 0, : flat.shape[2]].reshape(mask.shape)
    first = lambda a, b: jnp.where(side == 0, a, b)
    text = jnp.concatenate([first(keep, got[:2]), first(got[:2], keep)], axis=1)
    masks = jnp.stack([first(mask, got_mask), first(got_mask, mask)])
    bias = jnp.where(masks.astype(jnp.float32) > 0.5, 0.0, LOW).astype(jnp.float32).reshape(-1)
    pieces, have = text, 1
    while have < pairs:
        take = min(have, pairs - have)
        more = shifted(pieces[:, : take * 2 * text_rows], have)
        pieces, have = jnp.concatenate([pieces, more], axis=1), have + take
    place = jnp.arange(pairs * 2 * text_rows, dtype=jnp.int32)
    token = (pair - place // (2 * text_rows)) % pairs * (2 * text_rows) + place % (2 * text_rows)
    text_bias = jnp.where(token < text_len[0], 0.0, LOW).astype(jnp.float32)
    text_bias = jnp.broadcast_to(text_bias[:, None], (token.shape[0], TILE))

    def both_ways(x):
        half = x.shape[0] // 2
        before, after = shifted(x[half:], 1), shifted(x[:half], -1)
        return before, after

    k = spread(keys)
    k_before, k_after = both_ways(k)
    v = spread(values)
    v_before, v_after = both_ways(v)
    q = spread(queries)
    q, k, v = (x.reshape(ways * rows, part) for x in (q, k, v))
    sums, stats = local_attention(tiles, bias, q, k, v, pieces[0], pieces[1], text_bias)
    k_far = jnp.stack([x.reshape(-1, part) for x in (k_before, k_after)])
    v_far = jnp.stack([x.reshape(-1, part) for x in (v_before, v_after)])
    out = halo_attention(tiles, bias, q, k_far, v_far, sums, stats)
    out = exchange(out.reshape(ways, rows, part))
    return out.reshape(2, heads, rows, part).transpose(2, 1, 0, 3).reshape(rows, width)


def solution(mesh):
    in_specs = (
        P(AXES, None),
        P(AXES, None),
        P(AXES, None),
        P("frame", "head"),
        P("frame", "head"),
        P("frame", None),
        P("frame"),
        P(),
    )
    return jax.shard_map(
        body, mesh=mesh, in_specs=in_specs, out_specs=P(AXES, None), check_vma=False
    )
```

```python
import functools
import math

import jax
import jax.numpy as jnp
from jax import lax
from jax.experimental import pallas as pl
from jax.experimental.pallas import tpu as pltpu
from jax.sharding import PartitionSpec as P

HD = 128
TILE = 128
AXES = ("frame", "head")
SCALE = math.log2(math.e) / math.sqrt(HD)
LOW = -1e30
NT = (((1,), (1,)), ((), ()))
SMEM = pl.BlockSpec(memory_space=pltpu.SMEM)
ANY = pl.BlockSpec(memory_space=pl.ANY)
SMALL = pltpu.CompilerParams(vmem_limit_bytes=12 << 20)
LARGE = pltpu.CompilerParams(vmem_limit_bytes=24 << 20)


def weigh(queries, keys, biases):
    scores = lax.dot_general(keys, queries, NT, preferred_element_type=jnp.float32)
    key_tiles, query_tiles = keys.shape[0] // TILE, queries.shape[0] // TILE
    tops, totals, weights = [], [], []
    for t in range(query_tiles):
        blocks = [
            scores[u * TILE : (u + 1) * TILE, t * TILE : (t + 1) * TILE] + biases[u][t]
            for u in range(key_tiles)
        ]
        top = functools.reduce(jnp.maximum, blocks)
        top = jnp.max(top, axis=0, keepdims=True)
        parts = [jnp.exp2((block - top) * SCALE) for block in blocks]
        total = functools.reduce(jnp.add, parts)
        tops.append(top)
        totals.append(jnp.sum(total, axis=0, keepdims=True))
        weights.append(jnp.concatenate([p.astype(jnp.bfloat16) for p in parts], axis=0))
    join = lambda parts: jnp.concatenate(parts, axis=1)
    return join(weights), join(tops), join(totals)


def group(queries, keys, values_t, biases):
    weights, top, total = weigh(queries, keys, biases)
    return jnp.dot(values_t, weights, preferred_element_type=jnp.float32), top, total


def merge(one, two):
    top = jnp.maximum(one[1], two[1])
    first, second = jnp.exp2((one[1] - top) * SCALE), jnp.exp2((two[1] - top) * SCALE)
    return one[0] * first + two[0] * second, top, one[2] * first + two[2] * second


def flat(block):
    return block.reshape(-1, block.shape[-1])


def near_kernel(
    tiles,
    bias,
    q_ref,
    v_ref,
    k_ref,
    before_ref,
    after_ref,
    keep_ref,
    got_ref,
    text_ref,
    near_ref,
    far_ref,
    scale_ref,
):
    side = pl.program_id(1)
    half, rows = k_ref.shape[0] // 2, keep_ref.shape[1]
    own, other = pl.ds(side * half, half), pl.ds((1 - side) * half, half)
    queries = flat(q_ref[:, 0])
    at = lambda t, u: bias[side * 8 + t, u]
    span = range(tiles)
    own_bias = [[at(t, u) for t in span] for u in span]
    own_bias += [
        [text_ref[j * TILE : (j + 1) * TILE, :]] * tiles for j in range(text_ref.shape[0] // TILE)
    ]
    mine = group(
        queries,
        jnp.concatenate([flat(k_ref[own]), keep_ref[0], got_ref[0, :rows]], axis=0),
        jnp.concatenate([flat(v_ref[own, 0]), keep_ref[1], got_ref[1, :rows]], axis=0).T,
        own_bias,
    )
    near = group(
        queries,
        flat(k_ref[other]),
        flat(v_ref[other, 0]).T,
        [[at(t, tiles + u) for t in span] for u in span],
    )
    weights, far_top, far_total = weigh(
        queries,
        jnp.where(side == 0, flat(before_ref[...]), flat(after_ref[...])),
        [[at(t, 2 * tiles + u) for t in span] for u in span],
    )
    weighted, top, total = merge(mine, near)
    best = jnp.maximum(top, far_top)
    near_scale, far_scale = jnp.exp2((top - best) * SCALE), jnp.exp2((far_top - best) * SCALE)
    total = total * near_scale + far_total * far_scale
    near_ref[0, 0] = weighted * (near_scale / total)
    far_ref[0, 0] = weights
    scale_ref[0, 0] = far_scale / total


def far_kernel(before_ref, after_ref, near_ref, far_ref, scale_ref, out_ref):
    side = pl.program_id(1)
    values = jnp.where(side == 0, flat(before_ref[...]), flat(after_ref[...])).T
    far = jnp.dot(values, far_ref[0, 0], preferred_element_type=jnp.float32)
    out = near_ref[0, 0] + far * scale_ref[0, 0]
    out_ref[...] = out.T.astype(out_ref.dtype).reshape(out_ref.shape)


def near_attention(tiles, bias, vq, k, k_before, k_after, keep, got, text_bias):
    ways, _, rows, part = vq.shape
    heads, half, length = part // HD, ways // 2, tiles * TILE
    far = pl.BlockSpec((half, rows, HD), lambda h, s: (0, 0, h))
    at = lambda h, s: (h, s, 0, 0)
    return pl.pallas_call(
        functools.partial(near_kernel, tiles),
        grid=(heads, 2),
        in_specs=[
            SMEM,
            pl.BlockSpec((half, 1, rows, HD), lambda h, s: (s, 1, 0, h)),
            pl.BlockSpec((ways, 1, rows, HD), lambda h, s: (0, 0, 0, h)),
            pl.BlockSpec((ways, rows, HD), lambda h, s: (0, 0, h)),
            far,
            far,
            pl.BlockSpec((2, keep.shape[1], HD), lambda h, s: (0, 0, h)),
            pl.BlockSpec((2, got.shape[1], HD), lambda h, s: (0, 0, h)),
            pl.BlockSpec(text_bias.shape, lambda h, s: (0, 0)),
        ],
        out_specs=[
            pl.BlockSpec((1, 1, HD, length), at),
            pl.BlockSpec((1, 1, length, length), at),
            pl.BlockSpec((1, 1, 1, length), at),
        ],
        out_shape=[
            jax.ShapeDtypeStruct((heads, 2, HD, length), jnp.float32),
            jax.ShapeDtypeStruct((heads, 2, length, length), jnp.bfloat16),
            jax.ShapeDtypeStruct((heads, 2, 1, length), jnp.float32),
        ],
        compiler_params=LARGE,
    )(bias, vq, vq, k, k_before, k_after, keep, got, text_bias)


def far_attention(v_before, v_after, near, weights, scales):
    half, rows, part = v_before.shape
    heads, length = part // HD, half * rows
    far = pl.BlockSpec((half, rows, HD), lambda h, s: (0, 0, h))
    at = lambda h, s: (h, s, 0, 0)
    return pl.pallas_call(
        far_kernel,
        grid=(heads, 2),
        in_specs=[
            far,
            far,
            pl.BlockSpec((1, 1, HD, length), at),
            pl.BlockSpec((1, 1, length, length), at),
            pl.BlockSpec((1, 1, 1, length), at),
        ],
        out_specs=pl.BlockSpec((half, rows, HD), lambda h, s: (s, 0, h)),
        out_shape=jax.ShapeDtypeStruct((2 * half, rows, part), jnp.bfloat16),
        compiler_params=LARGE,
    )(v_before, v_after, near, weights, scales)


def split_kernel(order, count, *refs):
    out_ref = refs[-1]
    part = out_ref.shape[-1]
    for i, x_ref in enumerate(refs[:count]):
        for p, g in enumerate(order):
            if count == 1:
                out_ref[p] = x_ref[:, g * part : (g + 1) * part]
            else:
                out_ref[p, i] = x_ref[:, g * part : (g + 1) * part]


def join_kernel(order, x_ref, out_ref):
    part = x_ref.shape[2]
    for p, g in enumerate(order):
        out_ref[:, g * part : (g + 1) * part] = x_ref[p]


def split_heads(order, arrays, first=()):
    rows, width = arrays[0].shape
    ways, count = len(order), len(arrays)
    shape = (ways, count, rows, width // ways) if count > 1 else (ways, rows, width // ways)
    return pl.pallas_call(
        functools.partial(split_kernel, order, count),
        in_specs=[pl.BlockSpec()] * count + [ANY] * len(first),
        out_shape=jax.ShapeDtypeStruct(shape, jnp.bfloat16),
        compiler_params=SMALL,
    )(*arrays, *first)


def join_heads(x, order):
    ways, rows, part = x.shape
    return pl.pallas_call(
        functools.partial(join_kernel, order),
        out_shape=jax.ShapeDtypeStruct((rows, ways * part), x.dtype),
        compiler_params=SMALL,
    )(x)


def mask_kernel(tiles, place, list_ref, count_ref, k_ref, v_ref, mask_ref, text_ref):
    text_ref[0] = k_ref[...]
    text_ref[1] = v_ref[...]
    lane = lax.broadcasted_iota(jnp.int32, (tiles, TILE), 1)
    ids = jnp.where(lane < tiles, place[0] * tiles + lane, place[1] * tiles + lane - tiles)
    ids = jnp.where(lane < 2 * tiles, ids, place[2] * tiles + lane - 2 * tiles)
    mask = jnp.zeros((tiles, TILE), jnp.float32)
    for i in range(list_ref.shape[1]):
        hit = (list_ref[:, i : i + 1] == ids) & (count_ref[...] > i)
        mask = jnp.where(hit, 1.0, mask)
    spare = jnp.zeros((mask_ref.shape[0] - tiles, TILE), jnp.float32)
    mask_ref[...] = jnp.concatenate([mask, spare], axis=0).astype(jnp.bfloat16)


def turn_kernel(pieces, place, mask_ref, *refs):
    texts, (offer_ref, keep_ref) = refs[:pieces], refs[-2:]
    low = place[3] == 0
    part = offer_ref.shape[2]
    for i in range(2):
        one = jnp.concatenate([t[i, :, :part] for t in texts], axis=0)
        two = jnp.concatenate([t[i, :, part:] for t in texts], axis=0)
        offer_ref[i, : one.shape[0]] = jnp.where(low, two, one)
        keep_ref[i] = jnp.where(low, one, two)
    offer_ref[0, keep_ref.shape[1] :, 0:TILE] = mask_ref[...]


def halves_kernel(vq_ref, _, __, ___, low_ref, high_ref):
    half = low_ref.shape[0]
    low_ref[...] = vq_ref[:half, 0]
    high_ref[...] = vq_ref[half:, 0]


def bias_kernel(pairs, rows, place, mask_ref, got_ref, bias_ref, text_ref):
    low = place[3] == 0
    start = got_ref.shape[1] - mask_ref.shape[0]
    mine, theirs = mask_ref[...], got_ref[0, start:, 0:TILE]
    for i, block in enumerate((jnp.where(low, mine, theirs), jnp.where(low, theirs, mine))):
        block = block.astype(jnp.float32)[0:8]
        bias_ref[8 * i : 8 * i + 8, :] = jnp.where(block > 0.5, 0.0, LOW)
    spot = lax.broadcasted_iota(jnp.int32, text_ref.shape, 0)
    spread = pairs * rows
    side = jnp.where(spot < spread, place[3], 1 - place[3])
    spot = jnp.where(spot < spread, spot, spot - spread)
    pair = place[4] - spot // rows
    pair = jnp.where(pair < 0, pair + pairs, pair)
    token = (2 * pair + side) * rows + spot % rows
    text_ref[...] = jnp.where(token < place[5], 0.0, LOW)


def body(queries, keys, values, text_keys, text_values, lists, counts, text_len):
    slabs, heads = lax.axis_size("frame"), lax.axis_size("head")
    slab = lax.axis_index("frame")
    pair, side = slab // 2, slab % 2
    ways, pairs = 2 * heads, slabs // 2
    tiles = lists.shape[0]
    rows, width = queries.shape
    part = width // ways
    count = slabs * heads
    groups = [list(range(ways * i, ways * (i + 1))) for i in range(pairs)]
    order = [2 * h + x for x in range(2) for h in range(heads)]

    def shifted(x, by):
        return lax.ppermute(x, AXES, [(i, (i + by * ways) % count) for i in range(count)])

    def swapped(x):
        flip = lambda i: i // ways * ways + (i + heads) % ways
        return lax.ppermute(x, AXES, [(i, flip(i)) for i in range(count)])

    def exchange(x):
        return lax.all_to_all(
            x, AXES, split_axis=0, concat_axis=0, tiled=True, axis_index_groups=groups
        )

    k = exchange(split_heads(order, (keys,)))
    ahead, behind = (slab + 1) % slabs, (slab + slabs - 1) % slabs
    toward, away = jnp.where(side == 0, ahead, behind), jnp.where(side == 0, behind, ahead)
    place = jnp.stack([slab, toward, away, side, pair, text_len[0]]).astype(jnp.int32)
    text_rows = text_keys.shape[0]
    mask, text = pl.pallas_call(
        functools.partial(mask_kernel, tiles),
        in_specs=[SMEM] + [pl.BlockSpec()] * 4,
        out_shape=[
            jax.ShapeDtypeStruct((16, TILE), jnp.bfloat16),
            jax.ShapeDtypeStruct((2, *text_keys.shape), jnp.bfloat16),
        ],
        compiler_params=SMALL,
    )(place, lists, counts[:, None], text_keys, text_values)
    if pairs <= 4:
        texts = [text] + [shifted(text, by) for by in range(1, pairs)]
    else:
        have = 1
        while have < pairs:
            take = min(have, pairs - have)
            more = shifted(text[:, : take * text_rows], have)
            text, have = jnp.concatenate([text, more], axis=1), have + take
        texts = [text]
    all_text = pairs * text_rows
    offer, keep = pl.pallas_call(
        functools.partial(turn_kernel, len(texts)),
        in_specs=[SMEM] + [pl.BlockSpec()] * (1 + len(texts)),
        out_shape=[
            jax.ShapeDtypeStruct((2, all_text + mask.shape[0], part), jnp.bfloat16),
            jax.ShapeDtypeStruct((2, all_text, part), jnp.bfloat16),
        ],
        compiler_params=SMALL,
    )(place, mask, *texts)
    got = swapped(offer)

    bias, text_bias = pl.pallas_call(
        functools.partial(bias_kernel, pairs, text_rows),
        in_specs=[SMEM] + [pl.BlockSpec()] * 2,
        out_shape=[
            jax.ShapeDtypeStruct((16, TILE), jnp.float32),
            jax.ShapeDtypeStruct((2 * all_text, TILE), jnp.float32),
        ],
        compiler_params=SMALL,
    )(place, mask, got)

    k_before, k_after = shifted(k[heads:], 1), shifted(k[:heads], -1)
    vq = exchange(split_heads(order, (values, queries), (k, keep)))

    half = jax.ShapeDtypeStruct((heads, rows, part), jnp.bfloat16)
    v_low, v_high = pl.pallas_call(
        halves_kernel,
        in_specs=[pl.BlockSpec(), ANY, ANY, ANY],
        out_shape=[half, half],
        compiler_params=SMALL,
    )(vq, text_bias, k_before, k_after)
    v_before, v_after = shifted(v_high, 1), shifted(v_low, -1)
    partial = near_attention(tiles, bias, vq, k, k_before, k_after, keep, got, text_bias)
    out = far_attention(v_before, v_after, *partial)
    return join_heads(exchange(out), order)


def solution(mesh):
    in_specs = (
        P(AXES, None),
        P(AXES, None),
        P(AXES, None),
        P("frame", "head"),
        P("frame", "head"),
        P("frame", None),
        P("frame"),
        P(),
    )
    return jax.shard_map(
        body, mesh=mesh, in_specs=in_specs, out_specs=P(AXES, None), check_vma=False
    )
```

```python
import functools
import math

import jax
import jax.numpy as jnp
from jax import lax
from jax.experimental import pallas as pl
from jax.experimental.pallas import tpu as pltpu
from jax.sharding import PartitionSpec as P

HD = 128
TILE = 128
AXES = ("frame", "head")
SCALE = math.log2(math.e) / math.sqrt(HD)
LOW = -1e30
NT = (((1,), (1,)), ((), ()))
SMEM = pl.BlockSpec(memory_space=pltpu.SMEM)
ANY = pl.BlockSpec(memory_space=pl.ANY)
SMALL = pltpu.CompilerParams(vmem_limit_bytes=12 << 20)
LARGE = pltpu.CompilerParams(vmem_limit_bytes=24 << 20)


def far_memory(x):
    return pltpu.with_memory_space_constraint(x, pltpu.HBM)


def weigh(queries, keys, biases):
    scores = lax.dot_general(keys, queries, NT, preferred_element_type=jnp.float32)
    key_tiles, query_tiles = keys.shape[0] // TILE, queries.shape[0] // TILE
    tops, totals, weights = [], [], []
    for t in range(query_tiles):
        blocks = [
            scores[u * TILE : (u + 1) * TILE, t * TILE : (t + 1) * TILE] + biases[u][t]
            for u in range(key_tiles)
        ]
        top = functools.reduce(jnp.maximum, blocks)
        top = jnp.max(top, axis=0, keepdims=True)
        parts = [jnp.exp2((block - top) * SCALE) for block in blocks]
        total = functools.reduce(jnp.add, parts)
        tops.append(top)
        totals.append(jnp.sum(total, axis=0, keepdims=True))
        weights.append(jnp.concatenate([p.astype(jnp.bfloat16) for p in parts], axis=0))
    join = lambda parts: jnp.concatenate(parts, axis=1)
    return join(weights), join(tops), join(totals)


def group(queries, keys, values_t, biases):
    weights, top, total = weigh(queries, keys, biases)
    return jnp.dot(values_t, weights, preferred_element_type=jnp.float32), top, total


def merge(one, two):
    top = jnp.maximum(one[1], two[1])
    first, second = jnp.exp2((one[1] - top) * SCALE), jnp.exp2((two[1] - top) * SCALE)
    return one[0] * first + two[0] * second, top, one[2] * first + two[2] * second


def flat(block):
    return block.reshape(-1, block.shape[-1])


def near_kernel(
    tiles,
    bias,
    q_ref,
    v_ref,
    k_ref,
    before_ref,
    after_ref,
    text_ref,
    text_bias_ref,
    near_ref,
    far_ref,
    scale_ref,
):
    side = pl.program_id(1)
    half = k_ref.shape[0] // 2
    own, other = pl.ds(side * half, half), pl.ds((1 - side) * half, half)
    queries = flat(q_ref[:, 0])
    at = lambda t, u: bias[side * 8 + t, u]
    span = range(tiles)
    own_bias = [[at(t, u) for t in span] for u in span]
    own_bias += [
        [text_bias_ref[j * TILE : (j + 1) * TILE, :]] * tiles
        for j in range(text_bias_ref.shape[0] // TILE)
    ]
    mine = group(
        queries,
        jnp.concatenate([flat(k_ref[own]), text_ref[0]], axis=0),
        jnp.concatenate([flat(v_ref[own, 0]), text_ref[1]], axis=0).T,
        own_bias,
    )
    near = group(
        queries,
        flat(k_ref[other]),
        flat(v_ref[other, 0]).T,
        [[at(t, tiles + u) for t in span] for u in span],
    )
    weights, far_top, far_total = weigh(
        queries,
        jnp.where(side == 0, flat(before_ref[...]), flat(after_ref[...])),
        [[at(t, 2 * tiles + u) for t in span] for u in span],
    )
    weighted, top, total = merge(mine, near)
    best = jnp.maximum(top, far_top)
    near_scale, far_scale = jnp.exp2((top - best) * SCALE), jnp.exp2((far_top - best) * SCALE)
    total = total * near_scale + far_total * far_scale
    near_ref[0, 0] = weighted * (near_scale / total)
    far_ref[0, 0] = weights
    scale_ref[0, 0] = far_scale / total


def far_kernel(before_ref, after_ref, near_ref, far_ref, scale_ref, out_ref):
    side = pl.program_id(1)
    values = jnp.where(side == 0, flat(before_ref[...]), flat(after_ref[...])).T
    far = jnp.dot(values, far_ref[0, 0], preferred_element_type=jnp.float32)
    out = near_ref[0, 0] + far * scale_ref[0, 0]
    out_ref[...] = out.T.astype(out_ref.dtype).reshape(out_ref.shape)


def near_attention(tiles, bias, vq, k, k_before, k_after, text, text_bias):
    ways, _, rows, part = vq.shape
    heads, half, length = part // HD, ways // 2, tiles * TILE
    far = pl.BlockSpec((half, rows, HD), lambda h, s: (0, 0, h))
    at = lambda h, s: (h, s, 0, 0)
    return pl.pallas_call(
        functools.partial(near_kernel, tiles),
        grid=(heads, 2),
        in_specs=[
            SMEM,
            pl.BlockSpec((half, 1, rows, HD), lambda h, s: (s, 1, 0, h)),
            pl.BlockSpec((ways, 1, rows, HD), lambda h, s: (0, 0, 0, h)),
            pl.BlockSpec((ways, rows, HD), lambda h, s: (0, 0, h)),
            far,
            far,
            pl.BlockSpec((2, text.shape[1], HD), lambda h, s: (0, 0, h)),
            pl.BlockSpec(text_bias.shape, lambda h, s: (0, 0)),
        ],
        out_specs=[
            pl.BlockSpec((1, 1, HD, length), at),
            pl.BlockSpec((1, 1, length, length), at),
            pl.BlockSpec((1, 1, 1, length), at),
        ],
        out_shape=[
            jax.ShapeDtypeStruct((heads, 2, HD, length), jnp.float32),
            jax.ShapeDtypeStruct((heads, 2, length, length), jnp.bfloat16),
            jax.ShapeDtypeStruct((heads, 2, 1, length), jnp.float32),
        ],
        compiler_params=LARGE,
    )(bias, vq, vq, k, k_before, k_after, text, text_bias)


def far_attention(v_before, v_after, near, weights, scales):
    half, rows, part = v_before.shape
    heads, length = part // HD, half * rows
    far = pl.BlockSpec((half, rows, HD), lambda h, s: (0, 0, h))
    at = lambda h, s: (h, s, 0, 0)
    return pl.pallas_call(
        far_kernel,
        grid=(heads, 2),
        in_specs=[
            far,
            far,
            pl.BlockSpec((1, 1, HD, length), at),
            pl.BlockSpec((1, 1, length, length), at),
            pl.BlockSpec((1, 1, 1, length), at),
        ],
        out_specs=pl.BlockSpec((half, rows, HD), lambda h, s: (s, 0, h)),
        out_shape=jax.ShapeDtypeStruct((2 * half, rows, part), jnp.bfloat16),
        compiler_params=LARGE,
    )(v_before, v_after, near, weights, scales)


def split_kernel(order, count, *refs):
    arrays, (out_ref, held, came, left) = refs[:count], refs[count:]
    part = out_ref.shape[-1]
    slot = lambda ref, p, i: ref.at[p] if count == 1 else ref.at[p, i]
    reads = [
        [
            pltpu.make_async_copy(
                x_ref.at[:, g * part : (g + 1) * part], slot(held, p, i), came.at[p, i]
            )
            for i, x_ref in enumerate(arrays)
        ]
        for p, g in enumerate(order)
    ]
    writes = [
        pltpu.make_async_copy(held.at[p], out_ref.at[p], left.at[p]) for p in range(len(order))
    ]
    for row in reads:
        for copy in row:
            copy.start()
    for row, write in zip(reads, writes):
        for copy in row:
            copy.wait()
        write.start()
    for write in writes:
        write.wait()


def join_kernel(order, x_ref, out_ref):
    part = x_ref.shape[2]
    for p, g in enumerate(order):
        out_ref[:, g * part : (g + 1) * part] = x_ref[p]


def split_heads(order, arrays):
    rows, width = arrays[0].shape
    ways, count = len(order), len(arrays)
    shape = (ways, count, rows, width // ways) if count > 1 else (ways, rows, width // ways)
    return pl.pallas_call(
        functools.partial(split_kernel, order, count),
        in_specs=[ANY] * count,
        out_specs=ANY,
        out_shape=pltpu.HBM(shape, jnp.bfloat16),
        scratch_shapes=[
            pltpu.VMEM(shape, jnp.bfloat16),
            pltpu.SemaphoreType.DMA((ways, count)),
            pltpu.SemaphoreType.DMA((ways,)),
        ],
        compiler_params=SMALL,
    )(*(far_memory(x) for x in arrays))


def join_heads(x, order):
    ways, rows, part = x.shape
    return pl.pallas_call(
        functools.partial(join_kernel, order),
        out_shape=jax.ShapeDtypeStruct((rows, ways * part), x.dtype),
        compiler_params=SMALL,
    )(x)


def mask_kernel(tiles, place, count, list_hbm, k_ref, v_ref, mask_ref, text_ref, list_ref, sems):
    pairs = ((list_hbm, list_ref), (k_ref, text_ref.at[0]), (v_ref, text_ref.at[1]))
    copies = [pltpu.make_async_copy(a, b, sems.at[i]) for i, (a, b) in enumerate(pairs)]
    for copy in copies:
        copy.start()
    for copy in copies:
        copy.wait()
    row = lax.broadcasted_iota(jnp.int32, (tiles, TILE), 0)
    counts = jnp.zeros((tiles, TILE), jnp.int32)
    for t in range(tiles):
        counts = jnp.where(row == t, count[t], counts)
    lane = lax.broadcasted_iota(jnp.int32, (tiles, TILE), 1)
    ids = jnp.where(lane < tiles, place[0] * tiles + lane, place[1] * tiles + lane - tiles)
    ids = jnp.where(lane < 2 * tiles, ids, place[2] * tiles + lane - 2 * tiles)
    mask = jnp.zeros((tiles, TILE), jnp.float32)
    for i in range(list_ref.shape[1]):
        hit = (list_ref[:, i : i + 1] == ids) & (counts > i)
        mask = jnp.where(hit, 1.0, mask)
    spare = jnp.zeros((mask_ref.shape[0] - tiles, TILE), jnp.float32)
    mask_ref[...] = jnp.concatenate([mask, spare], axis=0).astype(jnp.bfloat16)


def turn_kernel(pieces, place, mask_ref, *refs):
    texts, (offer_ref, keep_ref, done_ref) = refs[:pieces], refs[-3:]
    done_ref[...] = jnp.zeros_like(done_ref)
    low = place[3] == 0
    part = offer_ref.shape[2]
    for i in range(2):
        one = jnp.concatenate([t[i, :, :part] for t in texts], axis=0)
        two = jnp.concatenate([t[i, :, part:] for t in texts], axis=0)
        offer_ref[i, : one.shape[0]] = jnp.where(low, two, one)
        keep_ref[i] = jnp.where(low, one, two)
    offer_ref[0, keep_ref.shape[1] :, 0:TILE] = mask_ref[...]


def halves_kernel(vq_ref, _, __, low_ref, high_ref):
    half = low_ref.shape[0]
    low_ref[...] = vq_ref[:half, 0]
    high_ref[...] = vq_ref[half:, 0]


def gate_kernel(*_):
    pass


def gated(x, *first):
    return pl.pallas_call(
        gate_kernel,
        in_specs=[ANY] * (1 + len(first)),
        out_specs=ANY,
        out_shape=pltpu.HBM(x.shape, x.dtype),
        input_output_aliases={0: 0},
        compiler_params=SMALL,
    )(far_memory(x), *first)


def bias_kernel(
    pairs, rows, place, mask_ref, keep_ref, got_ref, bias_ref, text_ref, all_ref
):
    low = place[3] == 0
    for i in range(2):
        all_ref[i] = jnp.concatenate([keep_ref[i], got_ref[i, : keep_ref.shape[1]]], axis=0)
    start = got_ref.shape[1] - mask_ref.shape[0]
    mine, theirs = mask_ref[...], got_ref[0, start:, 0:TILE]
    for i, block in enumerate((jnp.where(low, mine, theirs), jnp.where(low, theirs, mine))):
        block = block.astype(jnp.float32)[0:8]
        bias_ref[8 * i : 8 * i + 8, :] = jnp.where(block > 0.5, 0.0, LOW)
    spot = lax.broadcasted_iota(jnp.int32, text_ref.shape, 0)
    spread = pairs * rows
    side = jnp.where(spot < spread, place[3], 1 - place[3])
    spot = jnp.where(spot < spread, spot, spot - spread)
    pair = place[4] - spot // rows
    pair = jnp.where(pair < 0, pair + pairs, pair)
    token = (2 * pair + side) * rows + spot % rows
    text_ref[...] = jnp.where(token < place[5], 0.0, LOW)


def body(queries, keys, values, text_keys, text_values, lists, counts, text_len):
    slabs, heads = lax.axis_size("frame"), lax.axis_size("head")
    slab = lax.axis_index("frame")
    pair, side = slab // 2, slab % 2
    ways, pairs = 2 * heads, slabs // 2
    tiles = lists.shape[0]
    rows, width = queries.shape
    part = width // ways
    count = slabs * heads
    groups = [list(range(ways * i, ways * (i + 1))) for i in range(pairs)]
    order = [2 * h + x for x in range(2) for h in range(heads)]

    def shifted(x, by):
        return lax.ppermute(x, AXES, [(i, (i + by * ways) % count) for i in range(count)])

    def swapped(x):
        flip = lambda i: i // ways * ways + (i + heads) % ways
        return lax.ppermute(x, AXES, [(i, flip(i)) for i in range(count)])

    def exchange(x):
        return lax.all_to_all(
            x, AXES, split_axis=0, concat_axis=0, tiled=True, axis_index_groups=groups
        )

    k = exchange(split_heads(order, (keys,)))
    ahead, behind = (slab + 1) % slabs, (slab + slabs - 1) % slabs
    toward, away = jnp.where(side == 0, ahead, behind), jnp.where(side == 0, behind, ahead)
    place = jnp.stack([slab, toward, away, side, pair, text_len[0]]).astype(jnp.int32)
    text_rows = text_keys.shape[0]
    mask, text = pl.pallas_call(
        functools.partial(mask_kernel, tiles),
        in_specs=[SMEM, SMEM] + [ANY] * 3,
        out_shape=[
            jax.ShapeDtypeStruct((16, TILE), jnp.bfloat16),
            jax.ShapeDtypeStruct((2, *text_keys.shape), jnp.bfloat16),
        ],
        scratch_shapes=[pltpu.VMEM(lists.shape, jnp.int32), pltpu.SemaphoreType.DMA((3,))],
        compiler_params=SMALL,
    )(place, counts, far_memory(lists), far_memory(text_keys), far_memory(text_values))
    if pairs <= 4:
        texts = [text] + [shifted(text, by) for by in range(1, pairs)]
    else:
        have = 1
        while have < pairs:
            take = min(have, pairs - have)
            more = shifted(text[:, : take * text_rows], have)
            text, have = jnp.concatenate([text, more], axis=1), have + take
        texts = [text]
    all_text = pairs * text_rows
    offer, keep, turned = pl.pallas_call(
        functools.partial(turn_kernel, len(texts)),
        in_specs=[SMEM] + [pl.BlockSpec()] * (1 + len(texts)),
        out_shape=[
            pltpu.HBM((2, all_text + mask.shape[0], part), jnp.bfloat16),
            pltpu.HBM((2, all_text, part), jnp.bfloat16),
            pltpu.HBM((8, TILE), jnp.float32),
        ],
        compiler_params=SMALL,
    )(place, mask, *texts)
    got = swapped(offer)

    bias, text_bias, text = pl.pallas_call(
        functools.partial(bias_kernel, pairs, text_rows),
        in_specs=[SMEM] + [pl.BlockSpec()] * 3,
        out_shape=[
            pltpu.HBM((16, TILE), jnp.float32),
            pltpu.HBM((2 * all_text, TILE), jnp.float32),
            pltpu.HBM((2, 2 * all_text, part), jnp.bfloat16),
        ],
        compiler_params=SMALL,
    )(place, mask, keep, got)

    k_before, k_after = far_memory(shifted(k[heads:], 1)), far_memory(shifted(k[:heads], -1))
    vq = exchange(gated(split_heads(order, (values, queries)), k, turned))

    half = jax.ShapeDtypeStruct((heads, rows, part), jnp.bfloat16)
    v_low, v_high = pl.pallas_call(
        halves_kernel,
        in_specs=[pl.BlockSpec()] + [ANY] * 2,
        out_shape=[half, half],
        compiler_params=SMALL,
    )(vq, k_before, k_after)
    v_before, v_after = shifted(v_high, 1), shifted(v_low, -1)
    text, text_bias = far_memory(text), far_memory(text_bias)
    partial = near_attention(tiles, bias, vq, far_memory(k), k_before, k_after, text, text_bias)
    out = far_attention(v_before, v_after, *partial)
    return join_heads(exchange(out), order)


def solution(mesh):
    in_specs = (
        P(AXES, None),
        P(AXES, None),
        P(AXES, None),
        P("frame", "head"),
        P("frame", "head"),
        P("frame", None),
        P("frame"),
        P(),
    )
    return jax.shard_map(
        body, mesh=mesh, in_specs=in_specs, out_specs=P(AXES, None), check_vma=False
    )
```

```python
import functools
import math

import jax
import jax.numpy as jnp
from jax import lax
from jax.experimental import pallas as pl
from jax.experimental.pallas import tpu as pltpu
from jax.sharding import PartitionSpec as P

HD = 128
TILE = 128
AXES = ("frame", "head")
SCALE = math.log2(math.e) / math.sqrt(HD)
LOW = -1e30
FLOOR = -1e29
CHUNK = 3
NT = (((1,), (1,)), ((), ()))
SMEM = pl.BlockSpec(memory_space=pltpu.SMEM)
ANY = pl.BlockSpec(memory_space=pl.ANY)
SMALL = pltpu.CompilerParams(vmem_limit_bytes=12 << 20)
LARGE = pltpu.CompilerParams(vmem_limit_bytes=24 << 20)


def far_memory(x):
    return pltpu.with_memory_space_constraint(x, pltpu.HBM)


def weigh(scores, biases):
    key_tiles, query_tiles = scores.shape[0] // TILE, scores.shape[1] // TILE
    tops, totals, weights = [], [], []
    for t in range(query_tiles):
        blocks = [
            scores[u * TILE : (u + 1) * TILE, t * TILE : (t + 1) * TILE] for u in range(key_tiles)
        ]
        tops_of = [
            jnp.max(block + bias[t], axis=0, keepdims=True)
            if bias[t].ndim
            else jnp.max(block, axis=0, keepdims=True) + bias[t]
            for block, bias in zip(blocks, biases)
        ]
        top = jnp.maximum(functools.reduce(jnp.maximum, tops_of), FLOOR)
        parts = [
            jnp.exp2((block - (top - bias[t])) * SCALE) for block, bias in zip(blocks, biases)
        ]
        total = functools.reduce(jnp.add, parts)
        tops.append(top)
        totals.append(jnp.sum(total, axis=0, keepdims=True))
        weights.append(jnp.concatenate([p.astype(jnp.bfloat16) for p in parts], axis=0))
    join = lambda parts: jnp.concatenate(parts, axis=1)
    return join(weights), join(tops), join(totals)


def merge(one, two):
    top = jnp.maximum(one[1], two[1])
    first, second = jnp.exp2((one[1] - top) * SCALE), jnp.exp2((two[1] - top) * SCALE)
    return one[0] * first + two[0] * second, top, one[2] * first + two[2] * second


def flat(block):
    return block.reshape(-1, block.shape[-1])


def near_kernel(
    tiles,
    chunk,
    bias,
    q_ref,
    v_ref,
    k_ref,
    before_ref,
    after_ref,
    keep_ref,
    got_ref,
    add_ref,
    near_ref,
    far_ref,
    scale_ref,
):
    side = pl.program_id(1)
    half = k_ref.shape[0] // 2
    own, other = pl.ds(side * half, half), pl.ds((1 - side) * half, half)
    queries = flat(q_ref[:, 0])
    at = lambda t, u: bias[side * 8 + t, u]
    adds = [add_ref[j * TILE : (j + 1) * TILE, :] for j in range(add_ref.shape[0] // TILE)]
    keys = (
        jnp.concatenate([flat(k_ref[own]), keep_ref[0], got_ref[0]], axis=0),
        flat(k_ref[other]),
        jnp.where(side == 0, flat(before_ref[...]), flat(after_ref[...])),
    )
    values = (
        jnp.concatenate([flat(v_ref[own, 0]), keep_ref[1], got_ref[1]], axis=0).T,
        flat(v_ref[other, 0]).T,
    )
    works = [(c, g) for c in range(0, tiles, chunk) for g in range(3)]

    def scores_of(c, g):
        some = queries[c * TILE : (c + chunk) * TILE]
        return lax.dot_general(keys[g], some, NT, preferred_element_type=jnp.float32)

    ahead, done = scores_of(*works[0]), []
    for i, (c, g) in enumerate(works):
        scores = ahead
        if i + 1 < len(works):
            ahead = scores_of(*works[i + 1])
        biases = [[at(t, g * tiles + u) for t in range(c, c + chunk)] for u in range(tiles)]
        if g == 0:
            biases += [[add] * chunk for add in adds]
        weights, top, total = weigh(scores, biases)
        lanes = slice(c * TILE, (c + chunk) * TILE)
        if g < 2:
            weighted = jnp.dot(values[g], weights, preferred_element_type=jnp.float32)
            done.append((weighted, top, total))
        else:
            far_ref[0, 0, :, lanes] = weights
            weighted, near_top, near_total = merge(*done)
            best = jnp.maximum(near_top, top)
            near_scale = jnp.exp2((near_top - best) * SCALE)
            far_scale = jnp.exp2((top - best) * SCALE)
            whole = near_total * near_scale + total * far_scale
            near_ref[0, 0, :, lanes] = weighted * (near_scale / whole)
            scale_ref[0, 0, :, lanes] = far_scale / whole
            done = []


def far_kernel(before_ref, after_ref, near_ref, far_ref, scale_ref, out_ref):
    side = pl.program_id(1)
    values = jnp.where(side == 0, flat(before_ref[...]), flat(after_ref[...])).T
    far = jnp.dot(values, far_ref[0, 0], preferred_element_type=jnp.float32)
    out = near_ref[0, 0] + far * scale_ref[0, 0]
    out_ref[...] = out.T.astype(out_ref.dtype).reshape(out_ref.shape)


def near_attention(tiles, bias, vq, k, k_before, k_after, keep, got, add):
    ways, _, rows, part = vq.shape
    heads, half, length = part // HD, ways // 2, tiles * TILE
    far = pl.BlockSpec((half, rows, HD), lambda h, s: (0, 0, h))
    text = pl.BlockSpec((2, keep.shape[1], HD), lambda h, s: (0, 0, h))
    at = lambda h, s: (h, s, 0, 0)
    return pl.pallas_call(
        functools.partial(near_kernel, tiles, CHUNK if tiles % CHUNK == 0 else 1),
        grid=(heads, 2),
        in_specs=[
            SMEM,
            pl.BlockSpec((half, 1, rows, HD), lambda h, s: (s, 1, 0, h)),
            pl.BlockSpec((ways, 1, rows, HD), lambda h, s: (0, 0, 0, h)),
            pl.BlockSpec((ways, rows, HD), lambda h, s: (0, 0, h)),
            far,
            far,
            text,
            text,
            pl.BlockSpec(add.shape, lambda h, s: (0, 0)),
        ],
        out_specs=[
            pl.BlockSpec((1, 1, HD, length), at),
            pl.BlockSpec((1, 1, length, length), at),
            pl.BlockSpec((1, 1, 1, length), at),
        ],
        out_shape=[
            jax.ShapeDtypeStruct((heads, 2, HD, length), jnp.float32),
            jax.ShapeDtypeStruct((heads, 2, length, length), jnp.bfloat16),
            jax.ShapeDtypeStruct((heads, 2, 1, length), jnp.float32),
        ],
        compiler_params=LARGE,
    )(bias, vq, vq, k, k_before, k_after, keep, got, add)


def far_attention(v_before, v_after, near, weights, scales):
    half, rows, part = v_before.shape
    heads, length = part // HD, half * rows
    far = pl.BlockSpec((half, rows, HD), lambda h, s: (0, 0, h))
    at = lambda h, s: (h, s, 0, 0)
    return pl.pallas_call(
        far_kernel,
        grid=(heads, 2),
        in_specs=[
            far,
            far,
            pl.BlockSpec((1, 1, HD, length), at),
            pl.BlockSpec((1, 1, length, length), at),
            pl.BlockSpec((1, 1, 1, length), at),
        ],
        out_specs=pl.BlockSpec((half, rows, HD), lambda h, s: (s, 0, h)),
        out_shape=jax.ShapeDtypeStruct((2 * half, rows, part), jnp.bfloat16),
        compiler_params=LARGE,
    )(v_before, v_after, near, weights, scales)


def split_kernel(order, count, *refs):
    arrays, (out_ref, held, came, left) = refs[:count], refs[count:]
    part = out_ref.shape[-1]
    slot = lambda ref, p, i: ref.at[p] if count == 1 else ref.at[p, i]
    reads = [
        [
            pltpu.make_async_copy(
                x_ref.at[:, g * part : (g + 1) * part], slot(held, p, i), came.at[p, i]
            )
            for i, x_ref in enumerate(arrays)
        ]
        for p, g in enumerate(order)
    ]
    writes = [
        pltpu.make_async_copy(held.at[p], out_ref.at[p], left.at[p]) for p in range(len(order))
    ]
    for row in reads:
        for copy in row:
            copy.start()
    for row, write in zip(reads, writes):
        for copy in row:
            copy.wait()
        write.start()
    for write in writes:
        write.wait()


def join_kernel(order, *refs):
    parts, out_ref = refs[:-1], refs[-1]
    width = out_ref.shape[1] // len(order)
    for p, g in enumerate(order):
        at = g * width
        for ref in parts:
            out_ref[:, at : at + ref.shape[2]] = ref[p]
            at += ref.shape[2]


def split_heads(order, arrays):
    rows, width = arrays[0].shape
    ways, count = len(order), len(arrays)
    shape = (ways, count, rows, width // ways) if count > 1 else (ways, rows, width // ways)
    return pl.pallas_call(
        functools.partial(split_kernel, order, count),
        in_specs=[ANY] * count,
        out_specs=ANY,
        out_shape=pltpu.HBM(shape, jnp.bfloat16),
        scratch_shapes=[
            pltpu.VMEM(shape, jnp.bfloat16),
            pltpu.SemaphoreType.DMA((ways, count)),
            pltpu.SemaphoreType.DMA((ways,)),
        ],
        compiler_params=SMALL,
    )(*(far_memory(x) for x in arrays))


def join_heads(order, *parts):
    ways, rows, _ = parts[0].shape
    width = sum(x.shape[2] for x in parts)
    return pl.pallas_call(
        functools.partial(join_kernel, order),
        out_shape=jax.ShapeDtypeStruct((rows, ways * width), jnp.bfloat16),
        compiler_params=SMALL,
    )(*parts)


def mask_kernel(tiles, place, count, list_hbm, k_ref, v_ref, mask_ref, text_ref, list_ref, sems):
    pairs = ((list_hbm, list_ref), (k_ref, text_ref.at[0]), (v_ref, text_ref.at[1]))
    copies = [pltpu.make_async_copy(a, b, sems.at[i]) for i, (a, b) in enumerate(pairs)]
    for copy in copies:
        copy.start()
    for copy in copies:
        copy.wait()
    row = lax.broadcasted_iota(jnp.int32, (tiles, TILE), 0)
    counts = jnp.zeros((tiles, TILE), jnp.int32)
    for t in range(tiles):
        counts = jnp.where(row == t, count[t], counts)
    lane = lax.broadcasted_iota(jnp.int32, (tiles, TILE), 1)
    ids = jnp.where(lane < tiles, place[0] * tiles + lane, place[1] * tiles + lane - tiles)
    ids = jnp.where(lane < 2 * tiles, ids, place[2] * tiles + lane - 2 * tiles)
    mask = jnp.zeros((tiles, TILE), jnp.float32)
    for i in range(list_ref.shape[1]):
        hit = (list_ref[:, i : i + 1] == ids) & (counts > i)
        mask = jnp.where(hit, 1.0, mask)
    spare = jnp.zeros((mask_ref.shape[0] - tiles, TILE), jnp.float32)
    mask_ref[...] = jnp.concatenate([mask, spare], axis=0).astype(jnp.bfloat16)


def turn_kernel(pairs, pieces, place, mask_ref, their_ref, *refs):
    texts, (offer_ref, keep_ref, bias_ref, add_ref) = refs[:pieces], refs[pieces:]
    low = place[3] == 0
    part = offer_ref.shape[2]
    for i in range(2):
        one = jnp.concatenate([t[i, :, :part] for t in texts], axis=0)
        two = jnp.concatenate([t[i, :, part:] for t in texts], axis=0)
        offer_ref[i] = jnp.where(low, two, one)
        keep_ref[i] = jnp.where(low, one, two)
    mine, theirs = mask_ref[...], their_ref[...]
    for i, block in enumerate((jnp.where(low, mine, theirs), jnp.where(low, theirs, mine))):
        block = block.astype(jnp.float32)[0:8]
        bias_ref[8 * i : 8 * i + 8, :] = jnp.where(block > 0.5, 0.0, LOW)
    spread = keep_ref.shape[1]
    rows = spread // pairs
    spot = lax.broadcasted_iota(jnp.int32, add_ref.shape, 0)
    side = jnp.where(spot < spread, place[3], 1 - place[3])
    spot = jnp.where(spot < spread, spot, spot - spread)
    pair = place[4] - spot // rows
    pair = jnp.where(pair < 0, pair + pairs, pair)
    token = (2 * pair + side) * rows + spot % rows
    add_ref[...] = jnp.where(token < place[5], 0.0, LOW)


def halves_kernel(vq_ref, _, __, low_ref, high_ref):
    half = low_ref.shape[0]
    low_ref[...] = vq_ref[:half, 0]
    high_ref[...] = vq_ref[half:, 0]


def gate_kernel(*_):
    pass


def gated(x, *first):
    return pl.pallas_call(
        gate_kernel,
        in_specs=[ANY] * (1 + len(first)),
        out_specs=ANY,
        out_shape=pltpu.HBM(x.shape, x.dtype),
        input_output_aliases={0: 0},
        compiler_params=SMALL,
    )(far_memory(x), *first)


def body(queries, keys, values, text_keys, text_values, lists, counts, text_len):
    slabs, heads = lax.axis_size("frame"), lax.axis_size("head")
    slab = lax.axis_index("frame")
    pair, side = slab // 2, slab % 2
    ways, pairs = 2 * heads, slabs // 2
    tiles = lists.shape[0]
    rows, width = queries.shape
    part = width // ways
    count = slabs * heads
    groups = [list(range(ways * i, ways * (i + 1))) for i in range(pairs)]
    order = [2 * h + x for x in range(2) for h in range(heads)]

    def shifted(x, by):
        return lax.ppermute(x, AXES, [(i, (i + by * ways) % count) for i in range(count)])

    def swapped(x):
        flip = lambda i: i // ways * ways + (i + heads) % ways
        return lax.ppermute(x, AXES, [(i, flip(i)) for i in range(count)])

    def exchange(x):
        return lax.all_to_all(
            x, AXES, split_axis=0, concat_axis=0, tiled=True, axis_index_groups=groups
        )

    k = exchange(split_heads(order, (keys,)))
    ahead, behind = (slab + 1) % slabs, (slab + slabs - 1) % slabs
    toward, away = jnp.where(side == 0, ahead, behind), jnp.where(side == 0, behind, ahead)
    place = jnp.stack([slab, toward, away, side, pair, text_len[0]]).astype(jnp.int32)
    text_rows = text_keys.shape[0]
    mask, text = pl.pallas_call(
        functools.partial(mask_kernel, tiles),
        in_specs=[SMEM, SMEM] + [ANY] * 3,
        out_shape=[
            jax.ShapeDtypeStruct((16, TILE), jnp.bfloat16),
            jax.ShapeDtypeStruct((2, *text_keys.shape), jnp.bfloat16),
        ],
        scratch_shapes=[pltpu.VMEM(lists.shape, jnp.int32), pltpu.SemaphoreType.DMA((3,))],
        compiler_params=SMALL,
    )(place, counts, far_memory(lists), far_memory(text_keys), far_memory(text_values))
    if pairs <= 4:
        texts = [text] + [shifted(text, by) for by in range(1, pairs)]
    else:
        have = 1
        while have < pairs:
            take = min(have, pairs - have)
            more = shifted(text[:, : take * text_rows], have)
            text, have = jnp.concatenate([text, more], axis=1), have + take
        texts = [text]
    all_text = pairs * text_rows
    offer, keep, bias, add = pl.pallas_call(
        functools.partial(turn_kernel, pairs, len(texts)),
        in_specs=[SMEM] + [pl.BlockSpec()] * (2 + len(texts)),
        out_shape=[
            pltpu.HBM((2, all_text, part), jnp.bfloat16),
            pltpu.HBM((2, all_text, part), jnp.bfloat16),
            pltpu.HBM((16, TILE), jnp.float32),
            pltpu.HBM((2 * all_text, TILE), jnp.float32),
        ],
        compiler_params=SMALL,
    )(place, mask, swapped(mask), *texts)
    got, keep, add = far_memory(swapped(offer)), far_memory(keep), far_memory(add)

    k_before, k_after = far_memory(shifted(k[heads:], 1)), far_memory(shifted(k[:heads], -1))
    vq = exchange(gated(split_heads(order, (values, queries)), k, add))

    v_low, v_high = pl.pallas_call(
        halves_kernel,
        in_specs=[pl.BlockSpec()] + [ANY] * 2,
        out_shape=[jax.ShapeDtypeStruct((heads, rows, part), jnp.bfloat16)] * 2,
        compiler_params=SMALL,
    )(vq, k_before, k_after)
    v_before, v_after = shifted(v_high, 1), shifted(v_low, -1)
    partial = near_attention(tiles, bias, vq, far_memory(k), k_before, k_after, keep, got, add)
    return join_heads(order, exchange(far_attention(v_before, v_after, *partial)))


def solution(mesh):
    in_specs = (
        P(AXES, None),
        P(AXES, None),
        P(AXES, None),
        P("frame", "head"),
        P("frame", "head"),
        P("frame", None),
        P("frame"),
        P(),
    )
    return jax.shard_map(
        body, mesh=mesh, in_specs=in_specs, out_specs=P(AXES, None), check_vma=False
    )
```

```python
import functools
import math

import jax
import jax.numpy as jnp
from jax import lax
from jax.experimental import pallas as pl
from jax.experimental.pallas import tpu as pltpu
from jax.sharding import PartitionSpec as P

HD = 128
TILE = 128
AXES = ("frame", "head")
SCALE = math.log2(math.e) / math.sqrt(HD)
LOW = -1e30
FLOOR = -1e29
CHUNK = 3
NT = (((1,), (1,)), ((), ()))
SMEM = pl.BlockSpec(memory_space=pltpu.SMEM)
ANY = pl.BlockSpec(memory_space=pl.ANY)
SMALL = pltpu.CompilerParams(vmem_limit_bytes=12 << 20)
LARGE = pltpu.CompilerParams(vmem_limit_bytes=24 << 20)


def far_memory(x):
    return pltpu.with_memory_space_constraint(x, pltpu.HBM)


def weigh(scores, biases):
    key_tiles, query_tiles = scores.shape[0] // TILE, scores.shape[1] // TILE
    tops, totals, weights = [], [], []
    for t in range(query_tiles):
        blocks = [
            scores[u * TILE : (u + 1) * TILE, t * TILE : (t + 1) * TILE] for u in range(key_tiles)
        ]
        tops_of = [
            jnp.max(block + bias[t], axis=0, keepdims=True)
            if bias[t].ndim
            else jnp.max(block, axis=0, keepdims=True) + bias[t]
            for block, bias in zip(blocks, biases)
        ]
        top = jnp.maximum(functools.reduce(jnp.maximum, tops_of), FLOOR)
        parts = [
            jnp.exp2((block - (top - bias[t])) * SCALE) for block, bias in zip(blocks, biases)
        ]
        total = functools.reduce(jnp.add, parts)
        tops.append(top)
        totals.append(jnp.sum(total, axis=0, keepdims=True))
        weights.append(jnp.concatenate([p.astype(jnp.bfloat16) for p in parts], axis=0))
    join = lambda parts: jnp.concatenate(parts, axis=1)
    return join(weights), join(tops), join(totals)


def merge(one, two):
    top = jnp.maximum(one[1], two[1])
    first, second = jnp.exp2((one[1] - top) * SCALE), jnp.exp2((two[1] - top) * SCALE)
    return one[0] * first + two[0] * second, top, one[2] * first + two[2] * second


def flat(block):
    return block.reshape(-1, block.shape[-1])


def near_kernel(
    tiles,
    chunk,
    bias,
    q_ref,
    v_ref,
    k_ref,
    before_ref,
    after_ref,
    keep_ref,
    got_ref,
    add_ref,
    near_ref,
    far_ref,
    scale_ref,
):
    side = pl.program_id(1)
    half = k_ref.shape[0] // 2
    own, other = pl.ds(side * half, half), pl.ds((1 - side) * half, half)
    queries = flat(q_ref[:, 0])
    at = lambda t, u: bias[side * 8 + t, u]
    adds = [add_ref[j * TILE : (j + 1) * TILE, :] for j in range(add_ref.shape[0] // TILE)]
    keys = (
        jnp.concatenate([flat(k_ref[own]), keep_ref[0], got_ref[0]], axis=0),
        flat(k_ref[other]),
        jnp.where(side == 0, flat(before_ref[...]), flat(after_ref[...])),
    )
    values = (
        jnp.concatenate([flat(v_ref[own, 0]), keep_ref[1], got_ref[1]], axis=0).T,
        flat(v_ref[other, 0]).T,
    )
    works = [(c, g) for c in range(0, tiles, chunk) for g in range(3)]

    def scores_of(c, g):
        some = queries[c * TILE : (c + chunk) * TILE]
        return lax.dot_general(keys[g], some, NT, preferred_element_type=jnp.float32)

    ahead, done = scores_of(*works[0]), []
    for i, (c, g) in enumerate(works):
        scores = ahead
        if i + 1 < len(works):
            ahead = scores_of(*works[i + 1])
        biases = [[at(t, g * tiles + u) for t in range(c, c + chunk)] for u in range(tiles)]
        if g == 0:
            biases += [[add] * chunk for add in adds]
        weights, top, total = weigh(scores, biases)
        lanes = slice(c * TILE, (c + chunk) * TILE)
        if g < 2:
            weighted = jnp.dot(values[g], weights, preferred_element_type=jnp.float32)
            done.append((weighted, top, total))
        else:
            far_ref[0, 0, :, lanes] = weights
            weighted, near_top, near_total = merge(*done)
            best = jnp.maximum(near_top, top)
            near_scale = jnp.exp2((near_top - best) * SCALE)
            far_scale = jnp.exp2((top - best) * SCALE)
            whole = near_total * near_scale + total * far_scale
            near_ref[0, 0, :, lanes] = weighted * (near_scale / whole)
            scale_ref[0, 0, :, lanes] = far_scale / whole
            done = []


def far_kernel(place, before_ref, after_ref, near_ref, far_ref, scale_ref, *rest):
    outs, held = rest[:-1], rest[-1]
    half = len(outs) // 2
    for side, ref in enumerate((before_ref, after_ref)):
        far = jnp.dot(flat(ref[...]).T, far_ref[0, side], preferred_element_type=jnp.float32)
        out = near_ref[0, side] + far * scale_ref[0, side]
        out = out.T.astype(held.dtype)
        held[side * half : (side + 1) * half] = out.reshape(half, *held.shape[1:])
    for d, out_ref in enumerate(outs):
        out_ref[...] = held[place[6] ^ d]


def near_attention(tiles, bias, vq, k, k_before, k_after, keep, got, add):
    ways, _, rows, part = vq.shape
    heads, half, length = part // HD, ways // 2, tiles * TILE
    far = pl.BlockSpec((half, rows, HD), lambda h, s: (0, 0, h))
    text = pl.BlockSpec((2, keep.shape[1], HD), lambda h, s: (0, 0, h))
    at = lambda h, s: (h, s, 0, 0)
    return pl.pallas_call(
        functools.partial(near_kernel, tiles, CHUNK if tiles % CHUNK == 0 else 1),
        grid=(heads, 2),
        in_specs=[
            SMEM,
            pl.BlockSpec((half, 1, rows, HD), lambda h, s: (s, 1, 0, h)),
            pl.BlockSpec((ways, 1, rows, HD), lambda h, s: (0, 0, 0, h)),
            pl.BlockSpec((ways, rows, HD), lambda h, s: (0, 0, h)),
            far,
            far,
            text,
            text,
            pl.BlockSpec(add.shape, lambda h, s: (0, 0)),
        ],
        out_specs=[
            pl.BlockSpec((1, 1, HD, length), at),
            pl.BlockSpec((1, 1, length, length), at),
            pl.BlockSpec((1, 1, 1, length), at),
        ],
        out_shape=[
            jax.ShapeDtypeStruct((heads, 2, HD, length), jnp.float32),
            jax.ShapeDtypeStruct((heads, 2, length, length), jnp.bfloat16),
            jax.ShapeDtypeStruct((heads, 2, 1, length), jnp.float32),
        ],
        compiler_params=LARGE,
    )(bias, vq, vq, k, k_before, k_after, keep, got, add)


def far_attention(place, v_before, v_after, near, weights, scales):
    half, rows, part = v_before.shape
    heads, length = part // HD, half * rows
    far = pl.BlockSpec((half, rows, HD), lambda h: (0, 0, h))
    at = lambda h: (h, 0, 0, 0)
    return pl.pallas_call(
        far_kernel,
        grid=(heads,),
        in_specs=[
            SMEM,
            far,
            far,
            pl.BlockSpec((1, 2, HD, length), at),
            pl.BlockSpec((1, 2, length, length), at),
            pl.BlockSpec((1, 2, 1, length), at),
        ],
        out_specs=[pl.BlockSpec((rows, HD), lambda h: (0, h))] * (2 * half),
        out_shape=[jax.ShapeDtypeStruct((rows, part), jnp.bfloat16)] * (2 * half),
        scratch_shapes=[pltpu.VMEM((2 * half, rows, HD), jnp.bfloat16)],
        compiler_params=LARGE,
    )(place, v_before, v_after, near, weights, scales)


def split_kernel(order, count, *refs):
    arrays, (out_ref, held, came, left) = refs[:count], refs[count:]
    part = out_ref.shape[-1]
    slot = lambda ref, p, i: ref.at[p] if count == 1 else ref.at[p, i]
    reads = [
        [
            pltpu.make_async_copy(
                x_ref.at[:, g * part : (g + 1) * part], slot(held, p, i), came.at[p, i]
            )
            for i, x_ref in enumerate(arrays)
        ]
        for p, g in enumerate(order)
    ]
    writes = [
        pltpu.make_async_copy(held.at[p], out_ref.at[p], left.at[p]) for p in range(len(order))
    ]
    for row in reads:
        for copy in row:
            copy.start()
    for row, write in zip(reads, writes):
        for copy in row:
            copy.wait()
        write.start()
    for write in writes:
        write.wait()


def join_kernel(heads, which, place, *refs):
    out_ref = refs[-1]
    for d, ref in zip(which, refs[:-1]):
        part = ref.shape[1]
        owner = place[6] ^ d
        group_at = 2 * lax.rem(owner, heads) + lax.div(owner, heads)
        out_ref[:, pl.ds(pl.multiple_of(group_at * part, part), part)] = ref[...]


def split_heads(order, arrays):
    rows, width = arrays[0].shape
    ways, count = len(order), len(arrays)
    shape = (ways, count, rows, width // ways) if count > 1 else (ways, rows, width // ways)
    return pl.pallas_call(
        functools.partial(split_kernel, order, count),
        in_specs=[ANY] * count,
        out_specs=ANY,
        out_shape=pltpu.HBM(shape, jnp.bfloat16),
        scratch_shapes=[
            pltpu.VMEM(shape, jnp.bfloat16),
            pltpu.SemaphoreType.DMA((ways, count)),
            pltpu.SemaphoreType.DMA((ways,)),
        ],
        compiler_params=SMALL,
    )(*(far_memory(x) for x in arrays))


def join_heads(heads, place, which, parts):
    rows, part = parts[0].shape
    return pl.pallas_call(
        functools.partial(join_kernel, heads, which),
        in_specs=[SMEM] + [pl.BlockSpec()] * len(parts),
        out_shape=jax.ShapeDtypeStruct((rows, len(parts) * part), jnp.bfloat16),
        compiler_params=SMALL,
    )(place, *parts)


def mask_kernel(tiles, place, count, list_hbm, k_ref, v_ref, mask_ref, text_ref, list_ref, sems):
    pairs = ((list_hbm, list_ref), (k_ref, text_ref.at[0]), (v_ref, text_ref.at[1]))
    copies = [pltpu.make_async_copy(a, b, sems.at[i]) for i, (a, b) in enumerate(pairs)]
    for copy in copies:
        copy.start()
    for copy in copies:
        copy.wait()
    row = lax.broadcasted_iota(jnp.int32, (tiles, TILE), 0)
    counts = jnp.zeros((tiles, TILE), jnp.int32)
    for t in range(tiles):
        counts = jnp.where(row == t, count[t], counts)
    lane = lax.broadcasted_iota(jnp.int32, (tiles, TILE), 1)
    ids = jnp.where(lane < tiles, place[0] * tiles + lane, place[1] * tiles + lane - tiles)
    ids = jnp.where(lane < 2 * tiles, ids, place[2] * tiles + lane - 2 * tiles)
    mask = jnp.zeros((tiles, TILE), jnp.float32)
    for i in range(list_ref.shape[1]):
        hit = (list_ref[:, i : i + 1] == ids) & (counts > i)
        mask = jnp.where(hit, 1.0, mask)
    spare = jnp.zeros((mask_ref.shape[0] - tiles, TILE), jnp.float32)
    mask_ref[...] = jnp.concatenate([mask, spare], axis=0).astype(jnp.bfloat16)


def turn_kernel(pairs, pieces, place, mask_ref, their_ref, *refs):
    texts, (offer_ref, keep_ref, bias_ref, add_ref) = refs[:pieces], refs[pieces:]
    low = place[3] == 0
    part = offer_ref.shape[2]
    for i in range(2):
        one = jnp.concatenate([t[i, :, :part] for t in texts], axis=0)
        two = jnp.concatenate([t[i, :, part:] for t in texts], axis=0)
        offer_ref[i] = jnp.where(low, two, one)
        keep_ref[i] = jnp.where(low, one, two)
    mine, theirs = mask_ref[...], their_ref[...]
    for i, block in enumerate((jnp.where(low, mine, theirs), jnp.where(low, theirs, mine))):
        block = block.astype(jnp.float32)[0:8]
        bias_ref[8 * i : 8 * i + 8, :] = jnp.where(block > 0.5, 0.0, LOW)
    spread = keep_ref.shape[1]
    rows = spread // pairs
    spot = lax.broadcasted_iota(jnp.int32, add_ref.shape, 0)
    side = jnp.where(spot < spread, place[3], 1 - place[3])
    spot = jnp.where(spot < spread, spot, spot - spread)
    pair = place[4] - spot // rows
    pair = jnp.where(pair < 0, pair + pairs, pair)
    token = (2 * pair + side) * rows + spot % rows
    add_ref[...] = jnp.where(token < place[5], 0.0, LOW)


def halves_kernel(vq_ref, _, __, low_ref, high_ref):
    half = low_ref.shape[0]
    low_ref[...] = vq_ref[:half, 0]
    high_ref[...] = vq_ref[half:, 0]


def gate_kernel(*_):
    pass


def gated(x, *first):
    return pl.pallas_call(
        gate_kernel,
        in_specs=[ANY] * (1 + len(first)),
        out_specs=ANY,
        out_shape=pltpu.HBM(x.shape, x.dtype),
        input_output_aliases={0: 0},
        compiler_params=SMALL,
    )(far_memory(x), *first)


def body(queries, keys, values, text_keys, text_values, lists, counts, text_len):
    slabs, heads = lax.axis_size("frame"), lax.axis_size("head")
    slab = lax.axis_index("frame")
    pair, side = slab // 2, slab % 2
    ways, pairs = 2 * heads, slabs // 2
    tiles = lists.shape[0]
    rows, width = queries.shape
    part = width // ways
    count = slabs * heads
    groups = [list(range(ways * i, ways * (i + 1))) for i in range(pairs)]
    order = [2 * h + x for x in range(2) for h in range(heads)]

    def shifted(x, by):
        return lax.ppermute(x, AXES, [(i, (i + by * ways) % count) for i in range(count)])

    def swapped(x):
        flip = lambda i: i // ways * ways + (i + heads) % ways
        return lax.ppermute(x, AXES, [(i, flip(i)) for i in range(count)])

    def crossed(x, by):
        return lax.ppermute(x, AXES, [(i, i // ways * ways + (i % ways ^ by)) for i in range(count)])

    def exchange(x):
        return lax.all_to_all(
            x, AXES, split_axis=0, concat_axis=0, tiled=True, axis_index_groups=groups
        )

    k = exchange(split_heads(order, (keys,)))
    ahead, behind = (slab + 1) % slabs, (slab + slabs - 1) % slabs
    toward, away = jnp.where(side == 0, ahead, behind), jnp.where(side == 0, behind, ahead)
    me = side * heads + lax.axis_index("head")
    place = jnp.stack([slab, toward, away, side, pair, text_len[0], me]).astype(jnp.int32)
    text_rows = text_keys.shape[0]
    mask, text = pl.pallas_call(
        functools.partial(mask_kernel, tiles),
        in_specs=[SMEM, SMEM] + [ANY] * 3,
        out_shape=[
            jax.ShapeDtypeStruct((16, TILE), jnp.bfloat16),
            jax.ShapeDtypeStruct((2, *text_keys.shape), jnp.bfloat16),
        ],
        scratch_shapes=[pltpu.VMEM(lists.shape, jnp.int32), pltpu.SemaphoreType.DMA((3,))],
        compiler_params=SMALL,
    )(place, counts, far_memory(lists), far_memory(text_keys), far_memory(text_values))
    if pairs <= 4:
        texts = [text] + [shifted(text, by) for by in range(1, pairs)]
    else:
        have = 1
        while have < pairs:
            take = min(have, pairs - have)
            more = shifted(text[:, : take * text_rows], have)
            text, have = jnp.concatenate([text, more], axis=1), have + take
        texts = [text]
    all_text = pairs * text_rows
    offer, keep, bias, add = pl.pallas_call(
        functools.partial(turn_kernel, pairs, len(texts)),
        in_specs=[SMEM] + [pl.BlockSpec()] * (2 + len(texts)),
        out_shape=[
            pltpu.HBM((2, all_text, part), jnp.bfloat16),
            pltpu.HBM((2, all_text, part), jnp.bfloat16),
            pltpu.HBM((16, TILE), jnp.float32),
            pltpu.HBM((2 * all_text, TILE), jnp.float32),
        ],
        compiler_params=SMALL,
    )(place, mask, swapped(mask), *texts)
    got, keep, add = far_memory(swapped(offer)), far_memory(keep), far_memory(add)

    k_before, k_after = far_memory(shifted(k[heads:], 1)), far_memory(shifted(k[:heads], -1))
    vq = exchange(gated(split_heads(order, (values, queries)), k, add))

    v_low, v_high = pl.pallas_call(
        halves_kernel,
        in_specs=[pl.BlockSpec()] + [ANY] * 2,
        out_shape=[jax.ShapeDtypeStruct((heads, rows, part), jnp.bfloat16)] * 2,
        compiler_params=SMALL,
    )(vq, k_before, k_after)
    v_before, v_after = shifted(v_high, 1), shifted(v_low, -1)
    partial = near_attention(tiles, bias, vq, far_memory(k), k_before, k_after, keep, got, add)
    outs = far_attention(place, v_before, v_after, *partial)
    sends = sorted(range(1, ways), key=lambda d: (d % 2, -(d // 2).bit_count(), d))
    return join_heads(heads, place, [0] + sends, [outs[0]] + [crossed(outs[d], d) for d in sends])


def solution(mesh):
    in_specs = (
        P(AXES, None),
        P(AXES, None),
        P(AXES, None),
        P("frame", "head"),
        P("frame", "head"),
        P("frame", None),
        P("frame"),
        P(),
    )
    return jax.shard_map(
        body, mesh=mesh, in_specs=in_specs, out_specs=P(AXES, None), check_vma=False
    )
```

```python
import functools
import math

import jax
import jax.numpy as jnp
from jax import lax
from jax.experimental import pallas as pl
from jax.experimental.pallas import tpu as pltpu
from jax.sharding import PartitionSpec as P

HD = 128
TILE = 128
AXES = ("frame", "head")
SCALE = math.log2(math.e) / math.sqrt(HD)
LOW = -1e30
FLOOR = -1e29
CHUNK = 3
NT = (((1,), (1,)), ((), ()))
SMEM = pl.BlockSpec(memory_space=pltpu.SMEM)
ANY = pl.BlockSpec(memory_space=pl.ANY)
SMALL = pltpu.CompilerParams(vmem_limit_bytes=12 << 20)
LARGE = pltpu.CompilerParams(vmem_limit_bytes=24 << 20)


def far_memory(x):
    return pltpu.with_memory_space_constraint(x, pltpu.HBM)


def weigh(scores, biases):
    key_tiles, query_tiles = scores.shape[0] // TILE, scores.shape[1] // TILE
    tops, totals, weights = [], [], []
    for t in range(query_tiles):
        blocks = [
            scores[u * TILE : (u + 1) * TILE, t * TILE : (t + 1) * TILE] for u in range(key_tiles)
        ]
        tops_of = [
            jnp.max(block + bias[t], axis=0, keepdims=True)
            if bias[t].ndim
            else jnp.max(block, axis=0, keepdims=True) + bias[t]
            for block, bias in zip(blocks, biases)
        ]
        top = jnp.maximum(functools.reduce(jnp.maximum, tops_of), FLOOR)
        parts = [
            jnp.exp2((block - (top - bias[t])) * SCALE) for block, bias in zip(blocks, biases)
        ]
        total = functools.reduce(jnp.add, parts)
        tops.append(top)
        totals.append(jnp.sum(total, axis=0, keepdims=True))
        weights.append(jnp.concatenate([p.astype(jnp.bfloat16) for p in parts], axis=0))
    join = lambda parts: jnp.concatenate(parts, axis=1)
    return join(weights), join(tops), join(totals)


def merge(one, two):
    top = jnp.maximum(one[1], two[1])
    first, second = jnp.exp2((one[1] - top) * SCALE), jnp.exp2((two[1] - top) * SCALE)
    return one[0] * first + two[0] * second, top, one[2] * first + two[2] * second


def flat(block):
    return block.reshape(-1, block.shape[-1])


def near_kernel(
    tiles,
    chunk,
    bias,
    q_ref,
    v_ref,
    k_ref,
    before_ref,
    after_ref,
    keep_ref,
    got_ref,
    add_ref,
    near_ref,
    far_ref,
    scale_ref,
):
    side = pl.program_id(1)
    half = k_ref.shape[0] // 2
    own, other = pl.ds(side * half, half), pl.ds((1 - side) * half, half)
    queries = flat(q_ref[:, 0])
    at = lambda t, u: bias[side * 8 + t, u]
    adds = [add_ref[j * TILE : (j + 1) * TILE, :] for j in range(add_ref.shape[0] // TILE)]
    keys = (
        jnp.concatenate([flat(k_ref[own]), keep_ref[0], got_ref[0]], axis=0),
        flat(k_ref[other]),
        jnp.where(side == 0, flat(before_ref[...]), flat(after_ref[...])),
    )
    values = (
        jnp.concatenate([flat(v_ref[own, 0]), keep_ref[1], got_ref[1]], axis=0).T,
        flat(v_ref[other, 0]).T,
    )
    works = [(c, g) for c in range(0, tiles, chunk) for g in range(3)]

    def scores_of(c, g):
        some = queries[c * TILE : (c + chunk) * TILE]
        return lax.dot_general(keys[g], some, NT, preferred_element_type=jnp.float32)

    ahead, done = scores_of(*works[0]), []
    for i, (c, g) in enumerate(works):
        scores = ahead
        if i + 1 < len(works):
            ahead = scores_of(*works[i + 1])
        biases = [[at(t, g * tiles + u) for t in range(c, c + chunk)] for u in range(tiles)]
        if g == 0:
            biases += [[add] * chunk for add in adds]
        weights, top, total = weigh(scores, biases)
        lanes = slice(c * TILE, (c + chunk) * TILE)
        if g < 2:
            weighted = jnp.dot(values[g], weights, preferred_element_type=jnp.float32)
            done.append((weighted, top, total))
        else:
            far_ref[0, 0, :, lanes] = weights
            weighted, near_top, near_total = merge(*done)
            best = jnp.maximum(near_top, top)
            near_scale = jnp.exp2((near_top - best) * SCALE)
            far_scale = jnp.exp2((top - best) * SCALE)
            whole = near_total * near_scale + total * far_scale
            near_ref[0, 0, :, lanes] = weighted * (near_scale / whole)
            scale_ref[0, 0, :, lanes] = far_scale / whole
            done = []


def far_kernel(place, before_ref, after_ref, near_ref, far_ref, scale_ref, *rest):
    outs, held = rest[:-1], rest[-1]
    half = len(outs) // 2
    for side, ref in enumerate((before_ref, after_ref)):
        far = jnp.dot(flat(ref[...]).T, far_ref[0, side], preferred_element_type=jnp.float32)
        out = near_ref[0, side] + far * scale_ref[0, side]
        out = out.T.astype(held.dtype)
        held[side * half : (side + 1) * half] = out.reshape(half, *held.shape[1:])
    for d, out_ref in enumerate(outs):
        out_ref[...] = held[place[6] ^ d]


def near_attention(tiles, bias, vq, k, k_before, k_after, keep, got, add):
    ways, _, rows, part = vq.shape
    heads, half, length = part // HD, ways // 2, tiles * TILE
    far = pl.BlockSpec((half, rows, HD), lambda h, s: (0, 0, h))
    text = pl.BlockSpec((2, keep.shape[1], HD), lambda h, s: (0, 0, h))
    at = lambda h, s: (h, s, 0, 0)
    return pl.pallas_call(
        functools.partial(near_kernel, tiles, CHUNK if tiles % CHUNK == 0 else 1),
        grid=(heads, 2),
        in_specs=[
            SMEM,
            pl.BlockSpec((half, 1, rows, HD), lambda h, s: (s, 1, 0, h)),
            pl.BlockSpec((ways, 1, rows, HD), lambda h, s: (0, 0, 0, h)),
            pl.BlockSpec((ways, rows, HD), lambda h, s: (0, 0, h)),
            far,
            far,
            text,
            text,
            pl.BlockSpec(add.shape, lambda h, s: (0, 0)),
        ],
        out_specs=[
            pl.BlockSpec((1, 1, HD, length), at),
            pl.BlockSpec((1, 1, length, length), at),
            pl.BlockSpec((1, 1, 1, length), at),
        ],
        out_shape=[
            jax.ShapeDtypeStruct((heads, 2, HD, length), jnp.float32),
            jax.ShapeDtypeStruct((heads, 2, length, length), jnp.bfloat16),
            jax.ShapeDtypeStruct((heads, 2, 1, length), jnp.float32),
        ],
        compiler_params=LARGE,
    )(bias, vq, vq, k, k_before, k_after, keep, got, add)


def far_attention(place, v_before, v_after, near, weights, scales):
    half, rows, part = v_before.shape
    heads, length = part // HD, half * rows
    far = pl.BlockSpec((half, rows, HD), lambda h: (0, 0, h))
    at = lambda h: (h, 0, 0, 0)
    return pl.pallas_call(
        far_kernel,
        grid=(heads,),
        in_specs=[
            SMEM,
            far,
            far,
            pl.BlockSpec((1, 2, HD, length), at),
            pl.BlockSpec((1, 2, length, length), at),
            pl.BlockSpec((1, 2, 1, length), at),
        ],
        out_specs=[pl.BlockSpec((rows, HD), lambda h: (0, h))] * (2 * half),
        out_shape=[jax.ShapeDtypeStruct((rows, part), jnp.bfloat16)] * (2 * half),
        scratch_shapes=[pltpu.VMEM((2 * half, rows, HD), jnp.bfloat16)],
        compiler_params=LARGE,
    )(place, v_before, v_after, near, weights, scales)


def split_kernel(order, count, *refs):
    arrays, (out_ref, held, came, left) = refs[:count], refs[count:]
    part = out_ref.shape[-1]
    slot = lambda ref, p, i: ref.at[p] if count == 1 else ref.at[p, i]
    reads = [
        [
            pltpu.make_async_copy(
                x_ref.at[:, g * part : (g + 1) * part], slot(held, p, i), came.at[p, i]
            )
            for i, x_ref in enumerate(arrays)
        ]
        for p, g in enumerate(order)
    ]
    writes = [
        pltpu.make_async_copy(held.at[p], out_ref.at[p], left.at[p]) for p in range(len(order))
    ]
    for row in reads:
        for copy in row:
            copy.start()
    for row, write in zip(reads, writes):
        for copy in row:
            copy.wait()
        write.start()
    for write in writes:
        write.wait()


def join_kernel(heads, which, place, *refs):
    out_ref = refs[-1]
    for d, ref in zip(which, refs[:-1]):
        part = ref.shape[1]
        owner = place[6] ^ d
        group_at = 2 * lax.rem(owner, heads) + lax.div(owner, heads)
        out_ref[:, pl.ds(pl.multiple_of(group_at * part, part), part)] = ref[...]


def split_heads(order, arrays):
    rows, width = arrays[0].shape
    ways, count = len(order), len(arrays)
    shape = (ways, count, rows, width // ways) if count > 1 else (ways, rows, width // ways)
    return pl.pallas_call(
        functools.partial(split_kernel, order, count),
        in_specs=[ANY] * count,
        out_specs=ANY,
        out_shape=pltpu.HBM(shape, jnp.bfloat16),
        scratch_shapes=[
            pltpu.VMEM(shape, jnp.bfloat16),
            pltpu.SemaphoreType.DMA((ways, count)),
            pltpu.SemaphoreType.DMA((ways,)),
        ],
        compiler_params=SMALL,
    )(*(far_memory(x) for x in arrays))


def join_heads(heads, place, which, parts):
    rows, part = parts[0].shape
    return pl.pallas_call(
        functools.partial(join_kernel, heads, which),
        in_specs=[SMEM] + [pl.BlockSpec()] * len(parts),
        out_shape=jax.ShapeDtypeStruct((rows, len(parts) * part), jnp.bfloat16),
        compiler_params=SMALL,
    )(place, *parts)


def mask_kernel(tiles, place, count, list_hbm, k_ref, v_ref, mask_ref, text_ref, list_ref, sems):
    pairs = ((list_hbm, list_ref), (k_ref, text_ref.at[0]), (v_ref, text_ref.at[1]))
    copies = [pltpu.make_async_copy(a, b, sems.at[i]) for i, (a, b) in enumerate(pairs)]
    for copy in copies:
        copy.start()
    for copy in copies:
        copy.wait()
    row = lax.broadcasted_iota(jnp.int32, (tiles, TILE), 0)
    counts = jnp.zeros((tiles, TILE), jnp.int32)
    for t in range(tiles):
        counts = jnp.where(row == t, count[t], counts)
    lane = lax.broadcasted_iota(jnp.int32, (tiles, TILE), 1)
    ids = jnp.where(lane < tiles, place[0] * tiles + lane, place[1] * tiles + lane - tiles)
    ids = jnp.where(lane < 2 * tiles, ids, place[2] * tiles + lane - 2 * tiles)
    mask = jnp.zeros((tiles, TILE), jnp.float32)
    for i in range(list_ref.shape[1]):
        hit = (list_ref[:, i : i + 1] == ids) & (counts > i)
        mask = jnp.where(hit, 1.0, mask)
    spare = jnp.zeros((mask_ref.shape[0] - tiles, TILE), jnp.float32)
    mask_ref[...] = jnp.concatenate([mask, spare], axis=0).astype(jnp.bfloat16)


def turn_kernel(pairs, pieces, place, mask_ref, their_ref, *refs):
    texts, (offer_ref, keep_ref, bias_ref, add_ref) = refs[:pieces], refs[pieces:]
    low = place[3] == 0
    part = offer_ref.shape[2]
    for i in range(2):
        one = jnp.concatenate([t[i, :, :part] for t in texts], axis=0)
        two = jnp.concatenate([t[i, :, part:] for t in texts], axis=0)
        offer_ref[i] = jnp.where(low, two, one)
        keep_ref[i] = jnp.where(low, one, two)
    mine, theirs = mask_ref[...], their_ref[...]
    for i, block in enumerate((jnp.where(low, mine, theirs), jnp.where(low, theirs, mine))):
        block = block.astype(jnp.float32)[0:8]
        bias_ref[8 * i : 8 * i + 8, :] = jnp.where(block > 0.5, 0.0, LOW)
    spread = keep_ref.shape[1]
    rows = spread // pairs
    spot = lax.broadcasted_iota(jnp.int32, add_ref.shape, 0)
    side = jnp.where(spot < spread, place[3], 1 - place[3])
    spot = jnp.where(spot < spread, spot, spot - spread)
    pair = place[4] - spot // rows
    pair = jnp.where(pair < 0, pair + pairs, pair)
    token = (2 * pair + side) * rows + spot % rows
    add_ref[...] = jnp.where(token < place[5], 0.0, LOW)


def halves_kernel(vq_ref, _, low_ref, high_ref):
    half = low_ref.shape[0]
    low_ref[...] = vq_ref[:half, 0]
    high_ref[...] = vq_ref[half:, 0]


def gate_kernel(*_):
    pass


def gated(x, *first):
    return pl.pallas_call(
        gate_kernel,
        in_specs=[ANY] * (1 + len(first)),
        out_specs=ANY,
        out_shape=pltpu.HBM(x.shape, x.dtype),
        input_output_aliases={0: 0},
        compiler_params=SMALL,
    )(far_memory(x), *first)


def body(queries, keys, values, text_keys, text_values, lists, counts, text_len):
    slabs, heads = lax.axis_size("frame"), lax.axis_size("head")
    slab = lax.axis_index("frame")
    pair, side = slab // 2, slab % 2
    ways, pairs = 2 * heads, slabs // 2
    tiles = lists.shape[0]
    rows, width = queries.shape
    part = width // ways
    count = slabs * heads
    groups = [list(range(ways * i, ways * (i + 1))) for i in range(pairs)]
    order = [2 * h + x for x in range(2) for h in range(heads)]

    def shifted(x, by):
        return lax.ppermute(x, AXES, [(i, (i + by * ways) % count) for i in range(count)])

    def swapped(x):
        flip = lambda i: i // ways * ways + (i + heads) % ways
        return lax.ppermute(x, AXES, [(i, flip(i)) for i in range(count)])

    def crossed(x, by):
        return lax.ppermute(x, AXES, [(i, i // ways * ways + (i % ways ^ by)) for i in range(count)])

    def exchange(x):
        return lax.all_to_all(
            x, AXES, split_axis=0, concat_axis=0, tiled=True, axis_index_groups=groups
        )

    k = exchange(split_heads(order, (keys,)))
    ahead, behind = (slab + 1) % slabs, (slab + slabs - 1) % slabs
    toward, away = jnp.where(side == 0, ahead, behind), jnp.where(side == 0, behind, ahead)
    me = side * heads + lax.axis_index("head")
    place = jnp.stack([slab, toward, away, side, pair, text_len[0], me]).astype(jnp.int32)
    text_rows = text_keys.shape[0]
    mask, text = pl.pallas_call(
        functools.partial(mask_kernel, tiles),
        in_specs=[SMEM, SMEM] + [ANY] * 3,
        out_shape=[
            jax.ShapeDtypeStruct((16, TILE), jnp.bfloat16),
            jax.ShapeDtypeStruct((2, *text_keys.shape), jnp.bfloat16),
        ],
        scratch_shapes=[pltpu.VMEM(lists.shape, jnp.int32), pltpu.SemaphoreType.DMA((3,))],
        compiler_params=SMALL,
    )(place, counts, far_memory(lists), far_memory(text_keys), far_memory(text_values))
    if pairs <= 4:
        texts = [text] + [shifted(text, by) for by in range(1, pairs)]
    else:
        have = 1
        while have < pairs:
            take = min(have, pairs - have)
            more = shifted(text[:, : take * text_rows], have)
            text, have = jnp.concatenate([text, more], axis=1), have + take
        texts = [text]
    all_text = pairs * text_rows
    offer, keep, bias, add = pl.pallas_call(
        functools.partial(turn_kernel, pairs, len(texts)),
        in_specs=[SMEM] + [pl.BlockSpec()] * (2 + len(texts)),
        out_shape=[
            pltpu.HBM((2, all_text, part), jnp.bfloat16),
            pltpu.HBM((2, all_text, part), jnp.bfloat16),
            pltpu.HBM((16, TILE), jnp.float32),
            pltpu.HBM((2 * all_text, TILE), jnp.float32),
        ],
        compiler_params=SMALL,
    )(place, mask, swapped(mask), *texts)
    got, keep, add = far_memory(swapped(offer)), far_memory(keep), far_memory(add)

    k_before, k_after = far_memory(shifted(k[heads:], 1)), far_memory(shifted(k[:heads], -1))
    vq = exchange(gated(split_heads(order, (values, queries)), k, add))

    v_low, v_high = pl.pallas_call(
        halves_kernel,
        in_specs=[pl.BlockSpec(), ANY],
        out_shape=[jax.ShapeDtypeStruct((heads, rows, part), jnp.bfloat16)] * 2,
        compiler_params=SMALL,
    )(vq, k_before)
    v_before, v_after = shifted(v_high, 1), shifted(v_low, -1)
    partial = near_attention(tiles, bias, vq, far_memory(k), k_before, k_after, keep, got, add)
    outs = far_attention(place, v_before, v_after, *partial)
    sends = sorted(range(1, ways), key=lambda d: (d % 2, -(d // 2).bit_count(), d))
    return join_heads(heads, place, [0] + sends, [outs[0]] + [crossed(outs[d], d) for d in sends])


def solution(mesh):
    in_specs = (
        P(AXES, None),
        P(AXES, None),
        P(AXES, None),
        P("frame", "head"),
        P("frame", "head"),
        P("frame", None),
        P("frame"),
        P(),
    )
    return jax.shard_map(
        body, mesh=mesh, in_specs=in_specs, out_specs=P(AXES, None), check_vma=False
    )
```

```python
import functools
import math

import jax
import jax.numpy as jnp
from jax import lax
from jax.experimental import pallas as pl
from jax.experimental.pallas import tpu as pltpu
from jax.sharding import PartitionSpec as P

HD = 128
TILE = 128
AXES = ("frame", "head")
SCALE = math.log2(math.e) / math.sqrt(HD)
LOW = -1e30
FLOOR = -1e29
CHUNK = 3
NT = (((1,), (1,)), ((), ()))
SMEM = pl.BlockSpec(memory_space=pltpu.SMEM)
ANY = pl.BlockSpec(memory_space=pl.ANY)
SMALL = pltpu.CompilerParams(vmem_limit_bytes=12 << 20)
LARGE = pltpu.CompilerParams(vmem_limit_bytes=24 << 20)


def far_memory(x):
    return pltpu.with_memory_space_constraint(x, pltpu.HBM)


def weigh(scores, biases):
    key_tiles, query_tiles = scores.shape[0] // TILE, scores.shape[1] // TILE
    tops, totals, weights = [], [], []
    for t in range(query_tiles):
        blocks = [
            scores[u * TILE : (u + 1) * TILE, t * TILE : (t + 1) * TILE] for u in range(key_tiles)
        ]
        tops_of = [
            jnp.max(block + bias[t], axis=0, keepdims=True)
            if bias[t].ndim
            else jnp.max(block, axis=0, keepdims=True) + bias[t]
            for block, bias in zip(blocks, biases)
        ]
        top = jnp.maximum(functools.reduce(jnp.maximum, tops_of), FLOOR)
        parts = [
            jnp.exp2((block - (top - bias[t])) * SCALE) for block, bias in zip(blocks, biases)
        ]
        total = functools.reduce(jnp.add, parts)
        tops.append(top)
        totals.append(jnp.sum(total, axis=0, keepdims=True))
        weights.append(jnp.concatenate([p.astype(jnp.bfloat16) for p in parts], axis=0))
    join = lambda parts: jnp.concatenate(parts, axis=1)
    return join(weights), join(tops), join(totals)


def merge(one, two):
    top = jnp.maximum(one[1], two[1])
    first, second = jnp.exp2((one[1] - top) * SCALE), jnp.exp2((two[1] - top) * SCALE)
    return one[0] * first + two[0] * second, top, one[2] * first + two[2] * second


def flat(block):
    return block.reshape(-1, block.shape[-1])


def near_kernel(
    tiles,
    chunk,
    bias,
    q_ref,
    v_ref,
    k_ref,
    before_ref,
    after_ref,
    keep_ref,
    got_ref,
    add_ref,
    near_ref,
    far_ref,
    scale_ref,
):
    side = pl.program_id(1)
    half = k_ref.shape[0] // 2
    own, other = pl.ds(side * half, half), pl.ds((1 - side) * half, half)
    queries = flat(q_ref[:, 0])
    at = lambda t, u: bias[side * 8 + t, u]
    adds = [add_ref[j * TILE : (j + 1) * TILE, :] for j in range(add_ref.shape[0] // TILE)]
    keys = (
        jnp.concatenate([flat(k_ref[own]), keep_ref[0], got_ref[0]], axis=0),
        flat(k_ref[other]),
        jnp.where(side == 0, flat(before_ref[...]), flat(after_ref[...])),
    )
    values = (
        jnp.concatenate([flat(v_ref[own, 0]), keep_ref[1], got_ref[1]], axis=0).T,
        flat(v_ref[other, 0]).T,
    )
    works = [(c, g) for c in range(0, tiles, chunk) for g in range(3)]

    def scores_of(c, g):
        some = queries[c * TILE : (c + chunk) * TILE]
        return lax.dot_general(keys[g], some, NT, preferred_element_type=jnp.float32)

    ahead, done = scores_of(*works[0]), []
    for i, (c, g) in enumerate(works):
        scores = ahead
        if i + 1 < len(works):
            ahead = scores_of(*works[i + 1])
        biases = [[at(t, g * tiles + u) for t in range(c, c + chunk)] for u in range(tiles)]
        if g == 0:
            biases += [[add] * chunk for add in adds]
        weights, top, total = weigh(scores, biases)
        lanes = slice(c * TILE, (c + chunk) * TILE)
        if g < 2:
            weighted = jnp.dot(values[g], weights, preferred_element_type=jnp.float32)
            done.append((weighted, top, total))
        else:
            far_ref[0, 0, :, lanes] = weights
            weighted, near_top, near_total = merge(*done)
            best = jnp.maximum(near_top, top)
            near_scale = jnp.exp2((near_top - best) * SCALE)
            far_scale = jnp.exp2((top - best) * SCALE)
            whole = near_total * near_scale + total * far_scale
            near_ref[0, 0, :, lanes] = weighted * (near_scale / whole)
            scale_ref[0, 0, :, lanes] = far_scale / whole
            done = []


def far_kernel(place, before_ref, after_ref, near_ref, far_ref, scale_ref, *rest):
    outs, held = rest[:-1], rest[-1]
    half = len(outs) // 2
    for side, ref in enumerate((before_ref, after_ref)):
        far = jnp.dot(flat(ref[...]).T, far_ref[0, side], preferred_element_type=jnp.float32)
        out = near_ref[0, side] + far * scale_ref[0, side]
        out = out.T.astype(held.dtype)
        held[side * half : (side + 1) * half] = out.reshape(half, *held.shape[1:])
    for d, out_ref in enumerate(outs):
        out_ref[...] = held[place[6] ^ d]


def near_attention(tiles, bias, vq, k, k_before, k_after, keep, got, add):
    ways, _, rows, part = vq.shape
    heads, half, length = part // HD, ways // 2, tiles * TILE
    far = pl.BlockSpec((half, rows, HD), lambda h, s: (0, 0, h))
    text = pl.BlockSpec((2, keep.shape[1], HD), lambda h, s: (0, 0, h))
    at = lambda h, s: (h, s, 0, 0)
    return pl.pallas_call(
        functools.partial(near_kernel, tiles, CHUNK if tiles % CHUNK == 0 else 1),
        grid=(heads, 2),
        in_specs=[
            SMEM,
            pl.BlockSpec((half, 1, rows, HD), lambda h, s: (s, 1, 0, h)),
            pl.BlockSpec((ways, 1, rows, HD), lambda h, s: (0, 0, 0, h)),
            pl.BlockSpec((ways, rows, HD), lambda h, s: (0, 0, h)),
            far,
            far,
            text,
            text,
            pl.BlockSpec(add.shape, lambda h, s: (0, 0)),
        ],
        out_specs=[
            pl.BlockSpec((1, 1, HD, length), at),
            pl.BlockSpec((1, 1, length, length), at),
            pl.BlockSpec((1, 1, 1, length), at),
        ],
        out_shape=[
            jax.ShapeDtypeStruct((heads, 2, HD, length), jnp.float32),
            jax.ShapeDtypeStruct((heads, 2, length, length), jnp.bfloat16),
            jax.ShapeDtypeStruct((heads, 2, 1, length), jnp.float32),
        ],
        compiler_params=LARGE,
    )(bias, vq, vq, k, k_before, k_after, keep, got, add)


def far_attention(place, v_before, v_after, near, weights, scales):
    half, rows, part = v_before.shape
    heads, length = part // HD, half * rows
    far = pl.BlockSpec((half, rows, HD), lambda h: (0, 0, h))
    at = lambda h: (h, 0, 0, 0)
    return pl.pallas_call(
        far_kernel,
        grid=(heads,),
        in_specs=[
            SMEM,
            far,
            far,
            pl.BlockSpec((1, 2, HD, length), at),
            pl.BlockSpec((1, 2, length, length), at),
            pl.BlockSpec((1, 2, 1, length), at),
        ],
        out_specs=[pl.BlockSpec((rows, HD), lambda h: (0, h))] * (2 * half),
        out_shape=[jax.ShapeDtypeStruct((rows, part), jnp.bfloat16)] * (2 * half),
        scratch_shapes=[pltpu.VMEM((2 * half, rows, HD), jnp.bfloat16)],
        compiler_params=LARGE,
    )(place, v_before, v_after, near, weights, scales)


def split_kernel(order, count, *refs):
    arrays, (out_ref, held, came, left) = refs[:count], refs[count:]
    part = out_ref.shape[-1]
    slot = lambda ref, p, i: ref.at[p] if count == 1 else ref.at[p, i]
    reads = [
        [
            pltpu.make_async_copy(
                x_ref.at[:, g * part : (g + 1) * part], slot(held, p, i), came.at[p, i]
            )
            for i, x_ref in enumerate(arrays)
        ]
        for p, g in enumerate(order)
    ]
    writes = [
        pltpu.make_async_copy(held.at[p], out_ref.at[p], left.at[p]) for p in range(len(order))
    ]
    for row in reads:
        for copy in row:
            copy.start()
    for row, write in zip(reads, writes):
        for copy in row:
            copy.wait()
        write.start()
    for write in writes:
        write.wait()


def join_kernel(heads, which, place, *refs):
    out_ref = refs[-1]
    for d, ref in zip(which, refs[:-1]):
        part = ref.shape[1]
        owner = place[6] ^ d
        group_at = 2 * lax.rem(owner, heads) + lax.div(owner, heads)
        out_ref[:, pl.ds(pl.multiple_of(group_at * part, part), part)] = ref[...]


def split_heads(order, arrays):
    rows, width = arrays[0].shape
    ways, count = len(order), len(arrays)
    shape = (ways, count, rows, width // ways) if count > 1 else (ways, rows, width // ways)
    return pl.pallas_call(
        functools.partial(split_kernel, order, count),
        in_specs=[ANY] * count,
        out_specs=ANY,
        out_shape=pltpu.HBM(shape, jnp.bfloat16),
        scratch_shapes=[
            pltpu.VMEM(shape, jnp.bfloat16),
            pltpu.SemaphoreType.DMA((ways, count)),
            pltpu.SemaphoreType.DMA((ways,)),
        ],
        compiler_params=SMALL,
    )(*(far_memory(x) for x in arrays))


def join_heads(heads, place, which, parts):
    rows, part = parts[0].shape
    return pl.pallas_call(
        functools.partial(join_kernel, heads, which),
        in_specs=[SMEM] + [pl.BlockSpec()] * len(parts),
        out_shape=jax.ShapeDtypeStruct((rows, len(parts) * part), jnp.bfloat16),
        compiler_params=SMALL,
    )(place, *parts)


def mask_kernel(tiles, place, count, list_hbm, k_ref, v_ref, mask_ref, text_ref, list_ref, sems):
    pairs = ((list_hbm, list_ref), (k_ref, text_ref.at[0]), (v_ref, text_ref.at[1]))
    copies = [pltpu.make_async_copy(a, b, sems.at[i]) for i, (a, b) in enumerate(pairs)]
    for copy in copies:
        copy.start()
    for copy in copies:
        copy.wait()
    row = lax.broadcasted_iota(jnp.int32, (tiles, TILE), 0)
    counts = jnp.zeros((tiles, TILE), jnp.int32)
    for t in range(tiles):
        counts = jnp.where(row == t, count[t], counts)
    lane = lax.broadcasted_iota(jnp.int32, (tiles, TILE), 1)
    ids = jnp.where(lane < tiles, place[0] * tiles + lane, place[1] * tiles + lane - tiles)
    ids = jnp.where(lane < 2 * tiles, ids, place[2] * tiles + lane - 2 * tiles)
    mask = jnp.zeros((tiles, TILE), jnp.float32)
    for i in range(list_ref.shape[1]):
        hit = (list_ref[:, i : i + 1] == ids) & (counts > i)
        mask = jnp.where(hit, 1.0, mask)
    spare = jnp.zeros((mask_ref.shape[0] - tiles, TILE), jnp.float32)
    mask_ref[...] = jnp.concatenate([mask, spare], axis=0).astype(jnp.bfloat16)


def turn_kernel(pairs, pieces, place, mask_ref, their_ref, *refs):
    texts, (offer_ref, keep_ref, bias_ref, add_ref) = refs[:pieces], refs[pieces:]
    low = place[3] == 0
    part = offer_ref.shape[2]
    for i in range(2):
        one = jnp.concatenate([t[i, :, :part] for t in texts], axis=0)
        two = jnp.concatenate([t[i, :, part:] for t in texts], axis=0)
        offer_ref[i] = jnp.where(low, two, one)
        keep_ref[i] = jnp.where(low, one, two)
    mine, theirs = mask_ref[...], their_ref[...]
    for i, block in enumerate((jnp.where(low, mine, theirs), jnp.where(low, theirs, mine))):
        block = block.astype(jnp.float32)[0:8]
        bias_ref[8 * i : 8 * i + 8, :] = jnp.where(block > 0.5, 0.0, LOW)
    spread = keep_ref.shape[1]
    rows = spread // pairs
    spot = lax.broadcasted_iota(jnp.int32, add_ref.shape, 0)
    side = jnp.where(spot < spread, place[3], 1 - place[3])
    spot = jnp.where(spot < spread, spot, spot - spread)
    pair = place[4] - spot // rows
    pair = jnp.where(pair < 0, pair + pairs, pair)
    token = (2 * pair + side) * rows + spot % rows
    add_ref[...] = jnp.where(token < place[5], 0.0, LOW)


def halves_kernel(vq_ref, _, low_ref, high_ref):
    half = low_ref.shape[0]
    low_ref[...] = vq_ref[:half, 0]
    high_ref[...] = vq_ref[half:, 0]


def gate_kernel(*_):
    pass


def gated(x, *first):
    return pl.pallas_call(
        gate_kernel,
        in_specs=[ANY] * (1 + len(first)),
        out_specs=ANY,
        out_shape=pltpu.HBM(x.shape, x.dtype),
        input_output_aliases={0: 0},
        compiler_params=SMALL,
    )(far_memory(x), *first)


def body(queries, keys, values, text_keys, text_values, lists, counts, text_len):
    slabs, heads = lax.axis_size("frame"), lax.axis_size("head")
    slab = lax.axis_index("frame")
    pair, side = slab // 2, slab % 2
    ways, pairs = 2 * heads, slabs // 2
    tiles = lists.shape[0]
    rows, width = queries.shape
    part = width // ways
    count = slabs * heads
    groups = [list(range(ways * i, ways * (i + 1))) for i in range(pairs)]
    order = [2 * h + x for x in range(2) for h in range(heads)]

    def shifted(x, by):
        return lax.ppermute(x, AXES, [(i, (i + by * ways) % count) for i in range(count)])

    def swapped(x):
        flip = lambda i: i // ways * ways + (i + heads) % ways
        return lax.ppermute(x, AXES, [(i, flip(i)) for i in range(count)])

    def crossed(x, by):
        return lax.ppermute(x, AXES, [(i, i // ways * ways + (i % ways ^ by)) for i in range(count)])

    def exchange(x):
        return lax.all_to_all(
            x, AXES, split_axis=0, concat_axis=0, tiled=True, axis_index_groups=groups
        )

    k = exchange(split_heads(order, (keys,)))
    ahead, behind = (slab + 1) % slabs, (slab + slabs - 1) % slabs
    toward, away = jnp.where(side == 0, ahead, behind), jnp.where(side == 0, behind, ahead)
    me = side * heads + lax.axis_index("head")
    place = jnp.stack([slab, toward, away, side, pair, text_len[0], me]).astype(jnp.int32)
    text_rows = text_keys.shape[0]
    mask, text = pl.pallas_call(
        functools.partial(mask_kernel, tiles),
        in_specs=[SMEM, SMEM] + [ANY] * 3,
        out_shape=[
            jax.ShapeDtypeStruct((16, TILE), jnp.bfloat16),
            jax.ShapeDtypeStruct((2, *text_keys.shape), jnp.bfloat16),
        ],
        scratch_shapes=[pltpu.VMEM(lists.shape, jnp.int32), pltpu.SemaphoreType.DMA((3,))],
        compiler_params=SMALL,
    )(place, counts, far_memory(lists), far_memory(text_keys), far_memory(text_values))
    if pairs <= 4:
        texts = [text] + [shifted(text, by) for by in range(1, pairs)]
    else:
        have = 1
        while have < pairs:
            take = min(have, pairs - have)
            more = shifted(text[:, : take * text_rows], have)
            text, have = jnp.concatenate([text, more], axis=1), have + take
        texts = [text]
    all_text = pairs * text_rows
    offer, keep, bias, add = pl.pallas_call(
        functools.partial(turn_kernel, pairs, len(texts)),
        in_specs=[SMEM] + [pl.BlockSpec()] * (2 + len(texts)),
        out_shape=[
            pltpu.HBM((2, all_text, part), jnp.bfloat16),
            pltpu.HBM((2, all_text, part), jnp.bfloat16),
            pltpu.HBM((16, TILE), jnp.float32),
            pltpu.HBM((2 * all_text, TILE), jnp.float32),
        ],
        compiler_params=SMALL,
    )(place, mask, swapped(mask), *texts)
    got, keep, add = far_memory(swapped(offer)), far_memory(keep), far_memory(add)

    k_before, k_after = far_memory(shifted(k[heads:], 1)), far_memory(shifted(k[:heads], -1))
    vq = exchange(gated(split_heads(order, (values, queries)), k, add))

    v_low, v_high = pl.pallas_call(
        halves_kernel,
        in_specs=[pl.BlockSpec(), ANY],
        out_shape=[jax.ShapeDtypeStruct((heads, rows, part), jnp.bfloat16)] * 2,
        compiler_params=SMALL,
    )(vq, k_after)
    v_before, v_after = shifted(v_high, 1), shifted(v_low, -1)
    partial = near_attention(tiles, bias, vq, far_memory(k), k_before, k_after, keep, got, add)
    outs = far_attention(place, v_before, v_after, *partial)
    sends = sorted(range(1, ways), key=lambda d: (d % 2, -(d // 2).bit_count(), d))
    return join_heads(heads, place, [0] + sends, [outs[0]] + [crossed(outs[d], d) for d in sends])


def solution(mesh):
    in_specs = (
        P(AXES, None),
        P(AXES, None),
        P(AXES, None),
        P("frame", "head"),
        P("frame", "head"),
        P("frame", None),
        P("frame"),
        P(),
    )
    return jax.shard_map(
        body, mesh=mesh, in_specs=in_specs, out_specs=P(AXES, None), check_vma=False
    )
```
